32 devices in a mesh: row: 4 (over z), col: 8 (over y, x, core).
Axes of the slice: x: 2, y: 2, z: 4, core: 2. Of those that a mesh axis runs over, the one named last changes fastest.
Arguments:
- item_table: float32 [1310720, 128], P(('row', 'col')), may hold values from -6 to 6
- owner_ids: int32 [4096, 50], P(('row', 'col')), may hold values from 0 to 31, as said below
- row_ids: int32 [4096, 50], P(('row', 'col')), may hold values from 0 to 40959
- lengths: int32 [4096], P(('row', 'col')), may hold values from 25 to 50
- dense_input: bfloat16 [4096, 256], P(('row', 'col')), may hold values from -6 to 6
- w_bottom: bfloat16 [256, 256], replicated, may hold values from -0.375 to 0.375
Outputs:
- features: float32 [4096, 384], P(('row', 'col'))
The draws below stay inside these ranges and needn't reach their ends.
Inputs may be any that keep to these rules, and one draw needn't show every extreme that they name: Among the live positions (p < lengths[u]) of the 128 users of one device, at most 300 have the same owner_ids value; in every draw some owner_ids values receive exactly 300 live positions from every device.
All inputs are finite; a program needn't handle non-finite values.
Results may differ from the reference program's by a relative error of at most 0.0003.
Values sent between devices are 32-bit elements; how exact they have to be, the bound alone decides.
A program may use at most 128 MiB of HBM per device.

```python
import jax
import jax.numpy as jnp
from jax import lax

DIM = 128
DENSE = 256
HIST = 50
ROWS_DEV = 40960
U_DEV = 128
OWNERS = 32
USERS = 4096
ITEMS = 1310720
CAP = 300
HOT = 2


def history_plan(key):
    seed_key = jax.random.fold_in(key, 7103)
    hot_owners = jax.random.permutation(jax.random.fold_in(seed_key, 1), OWNERS)[:HOT]
    hot_flag = jnp.zeros((OWNERS,), jnp.int32).at[hot_owners].set(1)
    hot_rows = jax.random.randint(jax.random.fold_in(seed_key, 2), (OWNERS, 16), 0, ROWS_DEV)
    slot_total = OWNERS * CAP
    pos_count = U_DEV * HIST

    def one_source(source):
        source_key = jax.random.fold_in(seed_key, 100 + source)
        lengths_dev = jax.random.randint(jax.random.fold_in(source_key, 1), (U_DEV,), HIST // 2, HIST + 1)
        position = lax.broadcasted_iota(jnp.int32, (U_DEV, HIST), 1)
        live_flag = (position < lengths_dev[:, None]).reshape(-1).astype(jnp.int32)
        slot_owner = jnp.arange(slot_total, dtype=jnp.int32) // CAP
        noise_part = jax.random.randint(jax.random.fold_in(source_key, 2), (slot_total,), 0, 1024)
        tiebreak = jax.random.permutation(jax.random.fold_in(source_key, 3), slot_total).astype(jnp.int32)
        slot_score = (noise_part + 2048 * hot_flag[slot_owner]) * slot_total + tiebreak
        chosen = lax.top_k(slot_score, pos_count)[1].astype(jnp.int32)
        live_first = (1 - live_flag) * pos_count + jax.random.permutation(jax.random.fold_in(source_key, 4), pos_count).astype(jnp.int32)
        ranked = jnp.argsort(live_first)
        owners_out = jnp.zeros((pos_count,), jnp.int32).at[ranked].set(chosen // CAP)
        hot_choice = jax.random.randint(jax.random.fold_in(source_key, 5), (pos_count,), 0, 16)
        hot_coin = jax.random.randint(jax.random.fold_in(source_key, 6), (pos_count,), 0, 4)
        uniform_row = jax.random.randint(jax.random.fold_in(source_key, 7), (pos_count,), 0, ROWS_DEV)
        rows_out = jnp.where(hot_coin == 0, hot_rows[owners_out, hot_choice], uniform_row)
        return (owners_out, rows_out.astype(jnp.int32), lengths_dev.astype(jnp.int32))
    return jax.vmap(one_source)(jnp.arange(OWNERS, dtype=jnp.int32))


def draw_owner_ids(key, part):
    owners_out, rows_out, lengths_all = history_plan(key)
    return owners_out.reshape(USERS, HIST)


def draw_row_ids(key, part):
    owners_out, rows_out, lengths_all = history_plan(key)
    return rows_out.reshape(USERS, HIST)


def draw_lengths(key, part):
    owners_out, rows_out, lengths_all = history_plan(key)
    return lengths_all.reshape(USERS)


def level_of(key, shape, pieces, least, top_value):
    loudness = 1.0
    for axis_at, blocks in pieces:
        steps = jax.random.uniform(jax.random.fold_in(jax.random.fold_in(key, 6), axis_at), (blocks,), jnp.float32, least / len(pieces), top_value / len(pieces))
        loudness = loudness * jnp.repeat(jnp.exp(steps), shape[axis_at] // blocks).reshape((-1,) + (1,) * (len(shape) - 1 - axis_at))
    return loudness


def scatter_about(stream_key, shape, width, bound, pieces=(), kind=jnp.bfloat16):
    entries = jax.random.normal(stream_key, shape, jnp.float32) * width
    if len(pieces) > 0:
        entries = level_of(stream_key, shape, pieces, -0.22, 0.18) * entries
    return jnp.clip(entries, min=-bound, max=bound).astype(kind)


def setup_inputs(seed: int = 0) -> dict:
    splits = jax.random.split(jax.random.key(seed), 7)
    return {
        "item_table": scatter_about(splits[0], (ITEMS, DIM), 1.0, 6.0, ((0, 32),), jnp.float32),
        "owner_ids": draw_owner_ids(jax.random.fold_in(splits[6], 71), 0),
        "row_ids": draw_row_ids(jax.random.fold_in(splits[6], 71), 0),
        "lengths": draw_lengths(jax.random.fold_in(splits[6], 71), 0),
        "dense_input": scatter_about(splits[4], (USERS, DENSE), 1.0, 6.0, ((0, 32),)),
        "w_bottom": scatter_about(splits[5], (DENSE, DENSE), DENSE ** -0.5, 0.375),
    }


def reference(item_table, owner_ids, row_ids, lengths, dense_input, w_bottom):
    item_index = (owner_ids * ROWS_DEV + row_ids).astype(jnp.int32)
    position = lax.broadcasted_iota(jnp.int32, owner_ids.shape, 1)
    live_mask = (position < lengths[:, None]).astype(item_table.dtype)
    index_blocks = item_index.reshape(USERS // U_DEV, U_DEV, HIST)
    mask_blocks = live_mask.reshape(USERS // U_DEV, U_DEV, HIST)

    def pool_block(bundle):
        index_block, mask_block = bundle
        gathered = jnp.take(item_table, index_block.reshape(-1), axis=0).reshape(U_DEV, HIST, DIM)
        return jnp.sum(gathered * mask_block[:, :, None], axis=1)

    totals = lax.map(pool_block, (index_blocks, mask_blocks)).reshape(USERS, DIM)
    pooled = totals / lengths[:, None].astype(jnp.float32)
    hidden = jnp.dot(dense_input, w_bottom, preferred_element_type=jnp.float32)
    return jnp.concatenate([pooled, jax.nn.silu(hidden)], axis=1)
```

```python
import functools

import jax
import jax.numpy as jnp
from jax import lax
from jax.experimental import pallas as pl
from jax.experimental.pallas import tpu as pltpu
from jax.sharding import PartitionSpec as P

MESH = pl.DeviceIdType.MESH
LANES = 128
SUBLANES = 8


def round_up(value, unit):
    return -(-value // unit) * unit


def drain(ref, sem):
    pltpu.make_async_copy(ref, ref, sem).wait()


def kernel(
    sizes,
    table_hbm, owner_ref, row_ref, len_ref, dense_ref, w_ref, out_ref,
    table, owner_live, acc, index_out, index_in, index_smem, gather0, gather1,
    send_c, total, recv_c, recv_ax, recv_ay, recv_by, recv_bx, recv_z,
    table_sem, index_send_sem, index_recv_sem, own_sem, smem_sem,
    send_c_sem, send_ax_sem, send_ay_sem, send_by_sem, send_bx_sem, send_z_sem,
    recv_c_sem, recv_ax_sem, recv_ay_sem, recv_by_sem, recv_bx_sem, recv_z_sem,
):
    nz, ncol, ny, nx, nc, cap = sizes
    owners = nz * ncol
    hist, users = owner_ref.shape
    half = users // 2
    width = acc.shape[1]
    tiles = width // LANES
    cap_rows = round_up(cap, 16)
    z = lax.axis_index("row")
    col = lax.axis_index("col")
    me = z * ncol + col
    c = col % nc
    x = (col // nc) % nx
    y = col // (nc * nx)

    def column(y_at, x_at, c_at):
        return (y_at * nx + x_at) * nc + c_at

    pieces = 8
    piece = table.shape[0] // pieces
    for at in range(pieces):
        rows = pl.ds(at * piece, piece)
        pltpu.make_async_copy(table_hbm.at[rows], table.at[rows], table_sem).start()

    barrier = pltpu.get_barrier_semaphore()

    @pl.loop(1, owners)
    def _(step):
        there = lax.rem(me + step, owners)
        pl.semaphore_signal(
            barrier, inc=1, device_id=(there // ncol, lax.rem(there, ncol)), device_id_type=MESH
        )

    lengths = len_ref[...]
    position = lax.broadcasted_iota(jnp.int32, (hist, users), 0)
    owner_live[...] = jnp.where(position < lengths, owner_ref[...], -1)
    owner_iota = lax.broadcasted_iota(jnp.int32, (owners, users), 0)

    def count(at, carry):
        return carry + jnp.where(owner_live[pl.ds(at, 1), :] == owner_iota, 1.0, 0.0)

    per_user = lax.fori_loop(0, hist, count, jnp.zeros((owners, users), jnp.float32), unroll=5)
    before = lax.broadcasted_iota(jnp.int32, (users, users), 0) < lax.broadcasted_iota(
        jnp.int32, (users, users), 1
    )
    offsets = jnp.dot(
        per_user.astype(jnp.bfloat16),
        jnp.where(before, 1.0, 0.0).astype(jnp.bfloat16),
        preferred_element_type=jnp.float32,
    )
    acc[...] = jnp.zeros_like(acc)
    slot_iota = lax.broadcasted_iota(jnp.int32, (cap_rows, users), 0).astype(jnp.float32)
    user_number = lax.broadcasted_iota(jnp.int32, (1, users), 1).astype(jnp.float32) + 1.0
    group = 5 if hist % 5 == 0 else 1

    def place(step, counts):
        left, right = [], []
        for k in range(group):
            at = step * group + k
            row_id = row_ref[pl.ds(at, 1), :]
            high = row_id // 256
            low = (row_id - high * 256).astype(jnp.float32)
            high = high.astype(jnp.float32)
            match = owner_live[pl.ds(at, 1), :] == owner_iota
            rank = jnp.sum(jnp.where(match, counts, 0.0), axis=0, keepdims=True)
            counts = counts + jnp.where(match, 1.0, 0.0)
            right.append(jnp.where(slot_iota == rank, 1.0, 0.0).astype(jnp.bfloat16))
            values = [jnp.where(match, v, 0.0) for v in (high, low, user_number)]
            left.append(jnp.concatenate(values, axis=0).astype(jnp.bfloat16))
        acc[:, :cap_rows] += lax.dot_general(
            jnp.concatenate(left, axis=1),
            jnp.concatenate(right, axis=1),
            (((1,), (1,)), ((), ())),
            preferred_element_type=jnp.float32,
        )
        return counts

    lax.fori_loop(0, hist // group, place, offsets)
    for at in range(tiles):
        lanes = slice(at * LANES, (at + 1) * LANES)
        rows = acc[0:owners, lanes] * 256.0 + acc[owners:2 * owners, lanes]
        index_out[:, at, :] = jnp.clip(rows.astype(jnp.int32), 0, table.shape[0] - 1)
        index_out[:, tiles + at, :] = acc[2 * owners:3 * owners, lanes].astype(jnp.int32)

    pl.semaphore_wait(barrier, owners - 1)

    @pl.loop(1, owners)
    def _(step):
        there = lax.rem(me + step, owners)
        pltpu.make_async_remote_copy(
            src_ref=index_out.at[there],
            dst_ref=index_in.at[me],
            send_sem=index_send_sem,
            recv_sem=index_recv_sem,
            device_id=(there // ncol, lax.rem(there, ncol)),
            device_id_type=MESH,
        ).start()

    own = pltpu.make_async_copy(index_out.at[me], index_in.at[me], own_sem)
    own.start()

    hidden = jnp.dot(dense_ref[...], w_ref[...], preferred_element_type=jnp.float32)
    dim = table.shape[1]
    out_ref[:, dim:] = hidden / (1.0 + jnp.exp(-hidden))
    gather0[...] = jnp.zeros_like(gather0)
    gather1[...] = jnp.zeros_like(gather1)

    own.wait()
    drain(index_in.at[pl.ds(0, owners - 1)], index_recv_sem)
    to_smem = pltpu.make_async_copy(index_in, index_smem, smem_sem)
    to_smem.start()
    to_smem.wait()
    drain(table, table_sem)

    user_iota = lax.broadcasted_iota(jnp.int32, (users, LANES), 0) + 1

    def block_sum(source, gathered):
        for slot in range(cap):
            row = index_smem[source, slot // LANES, slot % LANES]
            gathered[slot:slot + 1, :] = table[pl.ds(row, 1), :]
        names = [index_in[source, pl.ds(tiles + at, 1), :] for at in range(tiles)]
        select = jnp.concatenate(
            [jnp.where(name == user_iota, 1.0, 0.0).astype(jnp.bfloat16) for name in names], axis=1
        )
        values = gathered[...]
        high = values.astype(jnp.bfloat16)
        low = (values - high.astype(jnp.float32)).astype(jnp.bfloat16)
        both = jnp.dot(
            select, jnp.concatenate([high, low], axis=1), preferred_element_type=jnp.float32
        )
        return both[:, :dim] + both[:, dim:]

    def send(src, dst, send_sem, recv_sem, z_at, col_at):
        pltpu.make_async_remote_copy(
            src_ref=src, dst_ref=dst, send_sem=send_sem, recv_sem=recv_sem,
            device_id=(z_at, col_at), device_id_type=MESH,
        ).start()

    def handle(dx, dy, dz):
        zt = lax.rem(z + dz, nz)
        yt = lax.rem(y + dy, ny)
        xt = lax.rem(x + dx, nx)
        slot = (dy * nx + dx) * nz + dz
        base = zt * ncol + column(yt, xt, 0)
        send_c[slot] = block_sum(base + 1 - c, gather0)
        send(send_c.at[slot], recv_c.at[slot], send_c_sem, recv_c_sem.at[slot],
             z, column(y, x, 1 - c))
        mine = block_sum(base + c, gather1)
        drain(recv_c.at[slot], recv_c_sem.at[slot])
        mine = mine + recv_c[slot]
        first, second = mine[:half], mine[half:]
        if dx == 0:
            for k in range(nx - 1):
                at = (k * ny + dy) * nz + dz
                drain(recv_ax.at[at], recv_ax_sem.at[at])
                first = first + recv_ax[at]
            if dy == 0:
                for k in range(ny - 1):
                    at = k * nz + dz
                    drain(recv_ay.at[at], recv_ay_sem.at[at])
                    first = first + recv_ay[at]
        if dy == 0:
            for k in range(ny - 1):
                at = (k * nx + dx) * nz + dz
                drain(recv_by.at[at], recv_by_sem.at[at])
                second = second + recv_by[at]
            if dx == 0:
                for k in range(nx - 1):
                    at = k * nz + dz
                    drain(recv_bx.at[at], recv_bx_sem.at[at])
                    second = second + recv_bx[at]
        total[slot, :half] = first
        total[slot, half:] = second
        upper, lower = total.at[slot, pl.ds(0, half)], total.at[slot, pl.ds(half, half)]
        if dx:
            at = ((dx - 1) * ny + dy) * nz + dz
            send(upper, recv_ax.at[at], send_ax_sem, recv_ax_sem.at[at], z, column(y, xt, c))
        elif dy:
            at = (dy - 1) * nz + dz
            send(upper, recv_ay.at[at], send_ay_sem, recv_ay_sem.at[at], z, column(yt, x, c))
        if dy:
            at = ((dy - 1) * nx + dx) * nz + dz
            send(lower, recv_by.at[at], send_by_sem, recv_by_sem.at[at], z, column(yt, x, c))
        elif dx:
            at = (dx - 1) * nz + dz
            send(lower, recv_bx.at[at], send_bx_sem, recv_bx_sem.at[at], z, column(y, xt, c))

    groups = [(dx, dy) for dy in range(ny) for dx in range(nx)]
    groups.sort(key=lambda pair: -((pair[0] > 0) + (pair[1] > 0)))
    for dx, dy in groups[:-1]:

        @pl.loop(0, nz)
        def _(step):
            handle(dx, dy, lax.rem(step + 1, nz))

    @pl.loop(1, nz)
    def _(dz):
        handle(0, 0, dz)
        send(total.at[dz], recv_z.at[dz - 1], send_z_sem, recv_z_sem.at[dz - 1],
             lax.rem(z + dz, nz), col)

    handle(0, 0, 0)
    pooled = total[0]
    for k in range(nz - 1):
        drain(recv_z.at[k], recv_z_sem.at[k])
        pooled = pooled + recv_z[k]
    divisor = jnp.broadcast_to(lengths.astype(jnp.float32), (users, users)).T
    out_ref[:, :dim] = pooled / divisor[:, :1]

    drain(index_in.at[pl.ds(0, owners - 1)], index_send_sem)
    drain(send_c, send_c_sem)
    drain(recv_ax, send_ax_sem)
    drain(recv_ay, send_ay_sem)
    drain(recv_by, send_by_sem)
    drain(recv_bx, send_bx_sem)
    drain(recv_z, send_z_sem)


def per_device(nz, ncol, item_table, owner_ids, row_ids, lengths, dense_input, w_bottom):
    users, hist = owner_ids.shape
    rows, dim = item_table.shape
    owners = nz * ncol
    cap = 3 * users * hist // (2 * owners)
    width = round_up(cap, LANES)
    tile_rows = round_up(2 * (width // LANES), SUBLANES)
    nc, nx = 2, 2
    ny = ncol // (nc * nx)
    chips = nz * ny * nx
    half = users // 2
    ax, ay, by, bx = (nx - 1) * ny * nz, (ny - 1) * nz, (ny - 1) * nx * nz, (nx - 1) * nz
    dma = pltpu.SemaphoreType.DMA
    vmem = pl.BlockSpec(memory_space=pltpu.VMEM)

    def floats(*shape):
        return pltpu.VMEM(shape, jnp.float32)

    return pl.pallas_call(
        functools.partial(kernel, (nz, ncol, ny, nx, nc, cap)),
        out_shape=jax.ShapeDtypeStruct((users, dim + w_bottom.shape[1]), jnp.float32),
        in_specs=[pl.BlockSpec(memory_space=pl.ANY)] + [vmem] * 5,
        out_specs=vmem,
        scratch_shapes=[
            floats(rows, dim),
            pltpu.VMEM((hist, users), jnp.int32),
            floats(3 * owners, width),
            pltpu.VMEM((owners, tile_rows, LANES), jnp.int32),
            pltpu.VMEM((owners, tile_rows, LANES), jnp.int32),
            pltpu.SMEM((owners, tile_rows, LANES), jnp.int32),
            floats(width, dim),
            floats(width, dim),
            floats(chips, users, dim),
            floats(chips, users, dim),
            floats(chips, users, dim),
            floats(ax, half, dim),
            floats(ay, half, dim),
            floats(by, half, dim),
            floats(bx, half, dim),
            floats(nz - 1, users, dim),
        ]
        + [dma] * 11
        + [dma((chips,)), dma((ax,)), dma((ay,)), dma((by,)), dma((bx,)), dma((nz - 1,))],
        compiler_params=pltpu.CompilerParams(
            collective_id=0, has_side_effects=True, vmem_limit_bytes=56 * 1024 * 1024
        ),
    )(item_table, owner_ids.T, row_ids.T, lengths[None, :], dense_input, w_bottom)


def solution(mesh):
    in_specs = (
        P(("row", "col"), None),
        P(("row", "col"), None),
        P(("row", "col"), None),
        P(("row", "col")),
        P(("row", "col"), None),
        P(),
    )
    out_specs = P(("row", "col"), None)
    body = functools.partial(per_device, mesh.shape["row"], mesh.shape["col"])
    return jax.shard_map(
        body, mesh=mesh, in_specs=in_specs, out_specs=out_specs, check_vma=False
    )
```

```python
import functools

import jax
import jax.numpy as jnp
from jax import lax
from jax.experimental import pallas as pl
from jax.experimental.pallas import tpu as pltpu
from jax.sharding import PartitionSpec as P

MESH = pl.DeviceIdType.MESH
LANES = 128
SUBLANES = 8


def round_up(value, unit):
    return -(-value // unit) * unit


def drain(ref, sem):
    pltpu.make_async_copy(ref, ref, sem).wait()


def kernel(
    sizes,
    table_hbm, owner_hbm, row_hbm, len_hbm, dense_hbm, w_hbm, pooled_ref, silu_ref,
    owner_ref, row_ref, len_ref, dense_ref, w_ref,
    table, owner_live, acc, index_out, index_in, index_smem, gather0, gather1,
    send_c, total, recv_c, recv_ax, recv_ay, recv_by, recv_bx, recv_z,
    owner_sem, row_sem, len_sem, dense_sem, w_sem,
    table_sem, index_send_sem, index_recv_sem, own_sem, smem_sem,
    send_c_sem, send_ax_sem, send_ay_sem, send_by_sem, send_bx_sem, send_z_sem,
    recv_c_sem, recv_ax_sem, recv_ay_sem, recv_by_sem, recv_bx_sem, recv_z_sem,
):
    nz, ncol, ny, nx, nc, cap = sizes
    owners = nz * ncol
    hist, users = owner_ref.shape
    half = users // 2
    width = acc.shape[0]
    tiles = width // LANES
    cap_rows = round_up(cap, 16)
    z = lax.axis_index("row")
    col = lax.axis_index("col")
    me = z * ncol + col
    c = col % nc
    x = (col // nc) % nx
    y = col // (nc * nx)

    def column(y_at, x_at, c_at):
        return (y_at * nx + x_at) * nc + c_at

    small = [
        pltpu.make_async_copy(*refs)
        for refs in (
            (len_hbm, len_ref, len_sem), (owner_hbm, owner_ref, owner_sem),
            (row_hbm, row_ref, row_sem), (dense_hbm, dense_ref, dense_sem),
            (w_hbm, w_ref, w_sem),
        )
    ]
    for copy in small:
        copy.start()

    pieces = 8
    piece = table.shape[0] // pieces
    for at in range(pieces):
        rows = pl.ds(at * piece, piece)
        pltpu.make_async_copy(table_hbm.at[rows], table.at[rows], table_sem).start()

    barrier = pltpu.get_barrier_semaphore()

    @pl.loop(1, owners)
    def _(step):
        there = lax.rem(me + step, owners)
        pl.semaphore_signal(
            barrier, inc=1, device_id=(there // ncol, lax.rem(there, ncol)), device_id_type=MESH
        )

    for copy in small[:3]:
        copy.wait()
    lengths = len_ref[...]
    position = lax.broadcasted_iota(jnp.int32, (hist, users), 0)
    owner_live[...] = jnp.where(position < lengths, owner_ref[...], -1)
    owner_iota = lax.broadcasted_iota(jnp.int32, (owners, users), 0)

    def count(at, carry):
        return carry + jnp.where(owner_live[pl.ds(at, 1), :] == owner_iota, 1.0, 0.0)

    per_user = lax.fori_loop(0, hist, count, jnp.zeros((owners, users), jnp.float32), unroll=5)
    before = lax.broadcasted_iota(jnp.int32, (users, users), 0) < lax.broadcasted_iota(
        jnp.int32, (users, users), 1
    )
    offsets = jnp.dot(
        per_user.astype(jnp.bfloat16),
        jnp.where(before, 1.0, 0.0).astype(jnp.bfloat16),
        preferred_element_type=jnp.float32,
    )
    acc[...] = jnp.zeros_like(acc)
    slot_iota = lax.broadcasted_iota(jnp.int32, (cap_rows, users), 0).astype(jnp.float32)
    user_number = lax.broadcasted_iota(jnp.int32, (1, users), 1).astype(jnp.float32) + 1.0
    group = 5 if hist % 5 == 0 else 1

    def place(step, counts):
        left, right = [], []
        for k in range(group):
            at = step * group + k
            row_id = row_ref[pl.ds(at, 1), :]
            high = row_id // 256
            low = (row_id - high * 256).astype(jnp.float32)
            high = high.astype(jnp.float32)
            match = owner_live[pl.ds(at, 1), :] == owner_iota
            rank = jnp.sum(jnp.where(match, counts, 0.0), axis=0, keepdims=True)
            counts = counts + jnp.where(match, 1.0, 0.0)
            right.append(jnp.where(slot_iota == rank, 1.0, 0.0).astype(jnp.bfloat16))
            values = [jnp.where(match, v, 0.0) for v in (high, low, user_number)]
            left.append(jnp.concatenate(values, axis=0).astype(jnp.bfloat16))
        acc[:cap_rows, :3 * owners] += lax.dot_general(
            jnp.concatenate(right, axis=1),
            jnp.concatenate(left, axis=1),
            (((1,), (1,)), ((), ())),
            preferred_element_type=jnp.float32,
        )
        return counts

    lax.fori_loop(0, hist // group, place, offsets)
    for at in range(tiles):
        found = acc[at * LANES:(at + 1) * LANES, :].T
        rows = found[0:owners] * 256.0 + found[owners:2 * owners]
        index_out[:, at, :] = jnp.clip(rows.astype(jnp.int32), 0, table.shape[0] - 1)
        index_out[:, tiles + at, :] = found[2 * owners:3 * owners].astype(jnp.int32)

    pl.semaphore_wait(barrier, owners - 1)

    @pl.loop(1, owners)
    def _(step):
        there = lax.rem(me + step, owners)
        pltpu.make_async_remote_copy(
            src_ref=index_out.at[there],
            dst_ref=index_in.at[me],
            send_sem=index_send_sem,
            recv_sem=index_recv_sem,
            device_id=(there // ncol, lax.rem(there, ncol)),
            device_id_type=MESH,
        ).start()

    own = pltpu.make_async_copy(index_out.at[me], index_in.at[me], own_sem)
    own.start()

    for copy in small[3:]:
        copy.wait()
    hidden = jnp.dot(dense_ref[...], w_ref[...], preferred_element_type=jnp.float32)
    dim = pooled_ref.shape[1]
    silu_ref[...] = hidden / (1.0 + jnp.exp(-hidden))
    gather0[...] = jnp.zeros_like(gather0)
    gather1[...] = jnp.zeros_like(gather1)

    own.wait()
    drain(index_in.at[pl.ds(0, owners - 1)], index_recv_sem)
    to_smem = pltpu.make_async_copy(index_in, index_smem, smem_sem)
    to_smem.start()
    to_smem.wait()
    drain(table, table_sem)

    user_iota = lax.broadcasted_iota(jnp.int32, (users, LANES), 0) + 1

    batch = 16

    def fetch(source, gathered):
        for first in range(0, cap, batch):
            slots = range(first, min(first + batch, cap))
            found = [table[index_smem[source, slot // LANES, slot % LANES]] for slot in slots]
            for slot, row in zip(slots, found):
                gathered[slot:slot + 1, :] = row

    def block_sum(source, gathered):
        names = [index_in[source, pl.ds(tiles + at, 1), :] for at in range(tiles)]
        select = jnp.concatenate(
            [jnp.where(name == user_iota, 1.0, 0.0).astype(jnp.bfloat16) for name in names], axis=1
        )
        values = gathered[...]
        high = values.astype(jnp.bfloat16)
        low = (values - high.astype(jnp.float32)).astype(jnp.bfloat16)
        both = jnp.dot(
            select, jnp.concatenate([high, low], axis=1), preferred_element_type=jnp.float32
        )
        return both[:, :dim] + both[:, dim:]

    def send(src, dst, send_sem, recv_sem, z_at, col_at):
        pltpu.make_async_remote_copy(
            src_ref=src, dst_ref=dst, send_sem=send_sem, recv_sem=recv_sem,
            device_id=(z_at, col_at), device_id_type=MESH,
        ).start()

    def source_of(dx, dy, dz):
        return lax.rem(z + dz, nz) * ncol + column(lax.rem(y + dy, ny), lax.rem(x + dx, nx), 0)

    def handle(dx, dy, dz, following):
        yt = lax.rem(y + dy, ny)
        xt = lax.rem(x + dx, nx)
        slot = (dy * nx + dx) * nz + dz
        base = source_of(dx, dy, dz)
        send_c[slot] = block_sum(base + 1 - c, gather0)
        fetch(base + c, gather1)
        send(send_c.at[slot], recv_c.at[slot], send_c_sem, recv_c_sem.at[slot],
             z, column(y, x, 1 - c))
        total[slot] = block_sum(base + c, gather1)
        if following is not None:
            fetch(following + 1 - c, gather0)
        drain(recv_c.at[slot], recv_c_sem.at[slot])
        mine = total[slot] + recv_c[slot]
        first, second = mine[:half], mine[half:]
        if dx == 0:
            for k in range(nx - 1):
                at = (k * ny + dy) * nz + dz
                drain(recv_ax.at[at], recv_ax_sem.at[at])
                first = first + recv_ax[at]
            if dy == 0:
                for k in range(ny - 1):
                    at = k * nz + dz
                    drain(recv_ay.at[at], recv_ay_sem.at[at])
                    first = first + recv_ay[at]
        if dy == 0:
            for k in range(ny - 1):
                at = (k * nx + dx) * nz + dz
                drain(recv_by.at[at], recv_by_sem.at[at])
                second = second + recv_by[at]
            if dx == 0:
                for k in range(nx - 1):
                    at = k * nz + dz
                    drain(recv_bx.at[at], recv_bx_sem.at[at])
                    second = second + recv_bx[at]
        total[slot, :half] = first
        total[slot, half:] = second
        upper, lower = total.at[slot, pl.ds(0, half)], total.at[slot, pl.ds(half, half)]
        if dx:
            at = ((dx - 1) * ny + dy) * nz + dz
            send(upper, recv_ax.at[at], send_ax_sem, recv_ax_sem.at[at], z, column(y, xt, c))
        elif dy:
            at = (dy - 1) * nz + dz
            send(upper, recv_ay.at[at], send_ay_sem, recv_ay_sem.at[at], z, column(yt, x, c))
        if dy:
            at = ((dy - 1) * nx + dx) * nz + dz
            send(lower, recv_by.at[at], send_by_sem, recv_by_sem.at[at], z, column(yt, x, c))
        elif dx:
            at = (dx - 1) * nz + dz
            send(lower, recv_bx.at[at], send_bx_sem, recv_bx_sem.at[at], z, column(y, xt, c))

    groups = [(dx, dy) for dy in range(ny) for dx in range(nx)]
    groups.sort(key=lambda pair: -((pair[0] > 0) + (pair[1] > 0)))
    fetch(source_of(*groups[0], 1) + 1 - c, gather0)
    for (dx, dy), (later_dx, later_dy) in zip(groups[:-1], groups[1:]):

        @pl.loop(0, nz)
        def _(step):
            wrap = (step + 1) // nz
            following = source_of(
                dx + wrap * (later_dx - dx), dy + wrap * (later_dy - dy),
                lax.rem(step + 2, nz),
            )
            handle(dx, dy, lax.rem(step + 1, nz), following)

    @pl.loop(1, nz)
    def _(dz):
        handle(0, 0, dz, source_of(0, 0, lax.rem(dz + 1, nz)))
        send(total.at[dz], recv_z.at[dz - 1], send_z_sem, recv_z_sem.at[dz - 1],
             lax.rem(z + dz, nz), col)

    handle(0, 0, 0, None)
    pooled = total[0]
    for k in range(nz - 1):
        drain(recv_z.at[k], recv_z_sem.at[k])
        pooled = pooled + recv_z[k]
    divisor = jnp.broadcast_to(lengths.astype(jnp.float32), (users, users)).T
    pooled_ref[...] = pooled / divisor[:, :1]

    drain(index_in.at[pl.ds(0, owners - 1)], index_send_sem)
    drain(send_c, send_c_sem)
    drain(recv_ax, send_ax_sem)
    drain(recv_ay, send_ay_sem)
    drain(recv_by, send_by_sem)
    drain(recv_bx, send_bx_sem)
    drain(recv_z, send_z_sem)


def per_device(nz, ncol, item_table, owner_ids, row_ids, lengths, dense_input, w_bottom):
    users, hist = owner_ids.shape
    rows, dim = item_table.shape
    owners = nz * ncol
    cap = 3 * users * hist // (2 * owners)
    width = round_up(cap, LANES)
    tile_rows = round_up(2 * (width // LANES), SUBLANES)
    nc, nx = 2, 2
    ny = ncol // (nc * nx)
    chips = nz * ny * nx
    half = users // 2
    ax, ay, by, bx = (nx - 1) * ny * nz, (ny - 1) * nz, (ny - 1) * nx * nz, (nx - 1) * nz
    dma = pltpu.SemaphoreType.DMA
    vmem = pl.BlockSpec(memory_space=pltpu.VMEM)

    def floats(*shape):
        return pltpu.VMEM(shape, jnp.float32)

    pooled, dense_out = pl.pallas_call(
        functools.partial(kernel, (nz, ncol, ny, nx, nc, cap)),
        out_shape=[
            jax.ShapeDtypeStruct((users, dim), jnp.float32),
            jax.ShapeDtypeStruct((users, w_bottom.shape[1]), jnp.float32),
        ],
        in_specs=[pl.BlockSpec(memory_space=pl.ANY)] * 6,
        out_specs=[vmem, vmem],
        scratch_shapes=[
            pltpu.VMEM((hist, users), jnp.int32),
            pltpu.VMEM((hist, users), jnp.int32),
            pltpu.VMEM((1, users), jnp.int32),
            pltpu.VMEM(dense_input.shape, dense_input.dtype),
            pltpu.VMEM(w_bottom.shape, w_bottom.dtype),
            floats(rows, 1, dim),
            pltpu.VMEM((hist, users), jnp.int32),
            floats(width, round_up(3 * owners, LANES)),
            pltpu.VMEM((owners, tile_rows, LANES), jnp.int32),
            pltpu.VMEM((owners, tile_rows, LANES), jnp.int32),
            pltpu.SMEM((owners, tile_rows, LANES), jnp.int32),
            floats(width, dim),
            floats(width, dim),
            floats(chips, users, dim),
            floats(chips, users, dim),
            floats(chips, users, dim),
            floats(ax, half, dim),
            floats(ay, half, dim),
            floats(by, half, dim),
            floats(bx, half, dim),
            floats(nz - 1, users, dim),
        ]
        + [dma] * 16
        + [dma((chips,)), dma((ax,)), dma((ay,)), dma((by,)), dma((bx,)), dma((nz - 1,))],
        compiler_params=pltpu.CompilerParams(
            collective_id=0, has_side_effects=True, vmem_limit_bytes=56 * 1024 * 1024
        ),
    )(item_table[:, None, :], owner_ids.T, row_ids.T, lengths[None, :], dense_input, w_bottom)
    return jnp.concatenate([pooled, dense_out], axis=1)


def solution(mesh):
    in_specs = (
        P(("row", "col"), None),
        P(("row", "col"), None),
        P(("row", "col"), None),
        P(("row", "col")),
        P(("row", "col"), None),
        P(),
    )
    out_specs = P(("row", "col"), None)
    body = functools.partial(per_device, mesh.shape["row"], mesh.shape["col"])
    return jax.shard_map(
        body, mesh=mesh, in_specs=in_specs, out_specs=out_specs, check_vma=False
    )
```

```python
import functools

import jax
import jax.numpy as jnp
from jax import lax
from jax.experimental import pallas as pl
from jax.experimental.pallas import tpu as pltpu
from jax.sharding import PartitionSpec as P

MESH = pl.DeviceIdType.MESH
LANES = 128
SUBLANES = 8


def round_up(value, unit):
    return -(-value // unit) * unit


def drain(ref, sem):
    pltpu.make_async_copy(ref, ref, sem).wait()


def kernel(
    sizes,
    table_hbm, owner_hbm, row_hbm, len_hbm, dense_hbm, w_hbm, pooled_ref, silu_ref,
    owner_ref, row_ref, len_ref, dense_ref, w_ref,
    table, owner_live, acc, index_out, index_in, index_tile, index_smem, gather0, gather1,
    send_c, total, recv_c, recv_ax, recv_ay, recv_by, recv_bx, recv_z,
    owner_sem, row_sem, len_sem, dense_sem, w_sem,
    table_sem, index_send_sem, index_recv_sem, own_sem, smem_sem,
    send_c_sem, send_ax_sem, send_ay_sem, send_by_sem, send_bx_sem, send_z_sem,
    recv_c_sem, recv_ax_sem, recv_ay_sem, recv_by_sem, recv_bx_sem, recv_z_sem,
):
    nz, ncol, ny, nx, nc, cap = sizes
    owners = nz * ncol
    hist, users = owner_ref.shape
    half = users // 2
    width = acc.shape[0]
    tiles = width // LANES
    cap_rows = round_up(cap, 16)
    z = lax.axis_index("row")
    col = lax.axis_index("col")
    me = z * ncol + col
    c = col % nc
    x = (col // nc) % nx
    y = col // (nc * nx)

    def column(y_at, x_at, c_at):
        return (y_at * nx + x_at) * nc + c_at

    small = [
        pltpu.make_async_copy(*refs)
        for refs in (
            (len_hbm, len_ref, len_sem), (owner_hbm, owner_ref, owner_sem),
            (row_hbm, row_ref, row_sem), (dense_hbm, dense_ref, dense_sem),
            (w_hbm, w_ref, w_sem),
        )
    ]
    for copy in small:
        copy.start()

    pieces = 8
    piece = table.shape[0] // pieces
    for at in range(pieces):
        rows = pl.ds(at * piece, piece)
        pltpu.make_async_copy(table_hbm.at[rows], table.at[rows], table_sem).start()

    barrier = pltpu.get_barrier_semaphore()

    @pl.loop(1, owners)
    def _(step):
        there = lax.rem(me + step, owners)
        pl.semaphore_signal(
            barrier, inc=1, device_id=(there // ncol, lax.rem(there, ncol)), device_id_type=MESH
        )

    for copy in small[:3]:
        copy.wait()
    lengths = len_ref[...]
    position = lax.broadcasted_iota(jnp.int32, (hist, users), 0)
    owner_live[...] = jnp.where(position < lengths, owner_ref[...], -1)
    owner_iota = lax.broadcasted_iota(jnp.int32, (owners, users), 0)

    def count(at, carry):
        return carry + jnp.where(owner_live[pl.ds(at, 1), :] == owner_iota, 1.0, 0.0)

    per_user = lax.fori_loop(0, hist, count, jnp.zeros((owners, users), jnp.float32), unroll=5)
    before = lax.broadcasted_iota(jnp.int32, (users, users), 0) < lax.broadcasted_iota(
        jnp.int32, (users, users), 1
    )
    offsets = jnp.dot(
        per_user.astype(jnp.bfloat16),
        jnp.where(before, 1.0, 0.0).astype(jnp.bfloat16),
        preferred_element_type=jnp.float32,
    )
    acc[...] = jnp.zeros_like(acc)
    slot_iota = lax.broadcasted_iota(jnp.int32, (cap_rows, users), 0).astype(jnp.float32)
    user_number = lax.broadcasted_iota(jnp.int32, (1, users), 1).astype(jnp.float32) + 1.0
    group = 5 if hist % 5 == 0 else 1

    def place(step, counts):
        left, right = [], []
        for k in range(group):
            at = step * group + k
            row_id = row_ref[pl.ds(at, 1), :]
            high = row_id // 256
            low = (row_id - high * 256).astype(jnp.float32)
            high = high.astype(jnp.float32)
            match = owner_live[pl.ds(at, 1), :] == owner_iota
            rank = jnp.sum(jnp.where(match, counts, 0.0), axis=0, keepdims=True)
            counts = counts + jnp.where(match, 1.0, 0.0)
            right.append(jnp.where(slot_iota == rank, 1.0, 0.0).astype(jnp.bfloat16))
            values = [jnp.where(match, v, 0.0) for v in (high, low, user_number)]
            left.append(jnp.concatenate(values, axis=0).astype(jnp.bfloat16))
        acc[:cap_rows, :3 * owners] += lax.dot_general(
            jnp.concatenate(right, axis=1),
            jnp.concatenate(left, axis=1),
            (((1,), (1,)), ((), ())),
            preferred_element_type=jnp.float32,
        )
        return counts

    lax.fori_loop(0, hist // group, place, offsets)
    for at in range(tiles):
        found = acc[at * LANES:(at + 1) * LANES, :].T
        rows = found[0:owners] * 256.0 + found[owners:2 * owners]
        index_out[:, at, :] = rows.astype(jnp.int32)
        index_out[:, tiles + at, :] = found[2 * owners:3 * owners].astype(jnp.int32)

    pl.semaphore_wait(barrier, owners - 1)

    @pl.loop(1, owners)
    def _(step):
        there = lax.rem(me + step, owners)
        pltpu.make_async_remote_copy(
            src_ref=index_out.at[there],
            dst_ref=index_in.at[me],
            send_sem=index_send_sem,
            recv_sem=index_recv_sem,
            device_id=(there // ncol, lax.rem(there, ncol)),
            device_id_type=MESH,
        ).start()

    own = pltpu.make_async_copy(index_out.at[me], index_in.at[me], own_sem)
    own.start()

    for copy in small[3:]:
        copy.wait()
    hidden = jnp.dot(dense_ref[...], w_ref[...], preferred_element_type=jnp.float32)
    dim = pooled_ref.shape[1]
    silu_ref[...] = hidden / (1.0 + jnp.exp(-hidden))
    gather0[...] = jnp.zeros_like(gather0)
    gather1[...] = jnp.zeros_like(gather1)

    own.wait()
    drain(index_in.at[pl.ds(0, owners - 1)], index_recv_sem)
    row_ids = index_in[:, :tiles, :]
    lane_iota = lax.broadcasted_iota(jnp.int32, row_ids.shape, 2)
    index_tile[:, :tiles, :] = jnp.clip(row_ids >> 3, 0, table.shape[0] - 1)
    index_tile[:, tiles:2 * tiles, :] = (lane_iota - row_ids) & (SUBLANES - 1)
    to_smem = pltpu.make_async_copy(index_tile, index_smem, smem_sem)
    to_smem.start()
    to_smem.wait()
    drain(table, table_sem)

    user_iota = lax.broadcasted_iota(jnp.int32, (users, LANES), 0) + 1

    sublane = lax.broadcasted_iota(jnp.int32, (SUBLANES, dim), 0)

    def fetch(source, gathered):
        for first in range(0, cap_rows, SUBLANES):
            rows = None
            for k in range(SUBLANES):
                tile_at, lane = divmod(first + k, LANES)
                tile = table[index_smem[source, tile_at, lane]]
                moved = pltpu.roll(tile, index_smem[source, tiles + tile_at, lane], 0)
                rows = moved if k == 0 else jnp.where(sublane == k, moved, rows)
            gathered[first:first + SUBLANES, :] = rows

    def block_sum(source, gathered):
        names = [index_in[source, pl.ds(tiles + at, 1), :] for at in range(tiles)]
        select = jnp.concatenate(
            [jnp.where(name == user_iota, 1.0, 0.0).astype(jnp.bfloat16) for name in names], axis=1
        )
        values = gathered[...]
        high = values.astype(jnp.bfloat16)
        low = (values - high.astype(jnp.float32)).astype(jnp.bfloat16)
        both = jnp.dot(
            select, jnp.concatenate([high, low], axis=1), preferred_element_type=jnp.float32
        )
        return both[:, :dim] + both[:, dim:]

    def send(src, dst, send_sem, recv_sem, z_at, col_at):
        pltpu.make_async_remote_copy(
            src_ref=src, dst_ref=dst, send_sem=send_sem, recv_sem=recv_sem,
            device_id=(z_at, col_at), device_id_type=MESH,
        ).start()

    def source_of(dx, dy, dz):
        return lax.rem(z + dz, nz) * ncol + column(lax.rem(y + dy, ny), lax.rem(x + dx, nx), 0)

    def offsets_at(step):
        group = step // nz
        return nx - 1 - group % nx, ny - 1 - group // nx, (step + 1) % nz

    def handle(step, last):
        dx, dy, dz = offsets_at(step)
        yt, xt = lax.rem(y + dy, ny), lax.rem(x + dx, nx)
        slot = (dy * nx + dx) * nz + dz
        base = source_of(dx, dy, dz)
        send_c[slot] = block_sum(base + 1 - c, gather0)
        fetch(base + c, gather1)
        send(send_c.at[slot], recv_c.at[slot], send_c_sem, recv_c_sem.at[slot],
             z, column(y, x, 1 - c))
        total[slot] = block_sum(base + c, gather1)
        if not last:
            fetch(source_of(*offsets_at(step + 1)) + 1 - c, gather0)
        drain(recv_c.at[slot], recv_c_sem.at[slot])
        total[slot] += recv_c[slot]
        near_x, near_y = dx == 0, dy == 0
        both = jnp.logical_and(near_x, near_y)
        upper, lower = pl.ds(0, half), pl.ds(half, half)

        def add(part, landed, sem, at):
            drain(landed.at[at], sem.at[at])
            total[slot, part] += landed[at]

        @pl.when(near_x)
        def _():
            for k in range(nx - 1):
                add(upper, recv_ax, recv_ax_sem, (k * ny + dy) * nz + dz)

        @pl.when(near_y)
        def _():
            for k in range(ny - 1):
                add(lower, recv_by, recv_by_sem, (k * nx + dx) * nz + dz)

        @pl.when(both)
        def _():
            for k in range(ny - 1):
                add(upper, recv_ay, recv_ay_sem, k * nz + dz)
            for k in range(nx - 1):
                add(lower, recv_bx, recv_bx_sem, k * nz + dz)

        @pl.when(dx > 0)
        def _():
            at = ((dx - 1) * ny + dy) * nz + dz
            send(total.at[slot, upper], recv_ax.at[at], send_ax_sem, recv_ax_sem.at[at],
                 z, column(y, xt, c))

        @pl.when(dy > 0)
        def _():
            at = ((dy - 1) * nx + dx) * nz + dz
            send(total.at[slot, lower], recv_by.at[at], send_by_sem, recv_by_sem.at[at],
                 z, column(yt, x, c))

        @pl.when(jnp.logical_and(near_x, dy > 0))
        def _():
            at = (dy - 1) * nz + dz
            send(total.at[slot, upper], recv_ay.at[at], send_ay_sem, recv_ay_sem.at[at],
                 z, column(yt, x, c))

        @pl.when(jnp.logical_and(near_y, dx > 0))
        def _():
            at = (dx - 1) * nz + dz
            send(total.at[slot, lower], recv_bx.at[at], send_bx_sem, recv_bx_sem.at[at],
                 z, column(y, xt, c))

        @pl.when(jnp.logical_and(both, dz > 0))
        def _():
            send(total.at[dz], recv_z.at[dz - 1], send_z_sem, recv_z_sem.at[dz - 1],
                 lax.rem(z + dz, nz), col)

    chips = nz * ny * nx
    fetch(source_of(*offsets_at(0)) + 1 - c, gather0)

    @pl.loop(0, chips - 1)
    def _(step):
        handle(step, False)

    handle(jnp.int32(chips - 1), True)
    pooled = total[0]
    for k in range(nz - 1):
        drain(recv_z.at[k], recv_z_sem.at[k])
        pooled = pooled + recv_z[k]
    divisor = jnp.broadcast_to(lengths.astype(jnp.float32), (users, users)).T
    pooled_ref[...] = pooled / divisor[:, :1]

    drain(index_in.at[pl.ds(0, owners - 1)], index_send_sem)
    drain(send_c, send_c_sem)
    drain(recv_ax, send_ax_sem)
    drain(recv_ay, send_ay_sem)
    drain(recv_by, send_by_sem)
    drain(recv_bx, send_bx_sem)
    drain(recv_z, send_z_sem)


def per_device(nz, ncol, item_table, owner_ids, row_ids, lengths, dense_input, w_bottom):
    users, hist = owner_ids.shape
    rows, dim = item_table.shape
    owners = nz * ncol
    cap = 3 * users * hist // (2 * owners)
    width = round_up(cap, LANES)
    tile_rows = round_up(2 * (width // LANES), SUBLANES)
    nc, nx = 2, 2
    ny = ncol // (nc * nx)
    chips = nz * ny * nx
    half = users // 2
    ax, ay, by, bx = (nx - 1) * ny * nz, (ny - 1) * nz, (ny - 1) * nx * nz, (nx - 1) * nz
    dma = pltpu.SemaphoreType.DMA
    vmem = pl.BlockSpec(memory_space=pltpu.VMEM)

    def floats(*shape):
        return pltpu.VMEM(shape, jnp.float32)

    pooled, dense_out = pl.pallas_call(
        functools.partial(kernel, (nz, ncol, ny, nx, nc, cap)),
        out_shape=[
            jax.ShapeDtypeStruct((users, dim), jnp.float32),
            jax.ShapeDtypeStruct((users, w_bottom.shape[1]), jnp.float32),
        ],
        in_specs=[pl.BlockSpec(memory_space=pl.ANY)] * 6,
        out_specs=[vmem, vmem],
        scratch_shapes=[
            pltpu.VMEM((hist, users), jnp.int32),
            pltpu.VMEM((hist, users), jnp.int32),
            pltpu.VMEM((1, users), jnp.int32),
            pltpu.VMEM(dense_input.shape, dense_input.dtype),
            pltpu.VMEM(w_bottom.shape, w_bottom.dtype),
            floats(rows // SUBLANES, SUBLANES, dim),
            pltpu.VMEM((hist, users), jnp.int32),
            floats(width, round_up(3 * owners, LANES)),
            pltpu.VMEM((owners, tile_rows, LANES), jnp.int32),
            pltpu.VMEM((owners, tile_rows, LANES), jnp.int32),
            pltpu.VMEM((owners, tile_rows, LANES), jnp.int32),
            pltpu.SMEM((owners, tile_rows, LANES), jnp.int32),
            floats(width, dim),
            floats(width, dim),
            floats(chips, users, dim),
            floats(chips, users, dim),
            floats(chips, users, dim),
            floats(ax, half, dim),
            floats(ay, half, dim),
            floats(by, half, dim),
            floats(bx, half, dim),
            floats(nz - 1, users, dim),
        ]
        + [dma] * 16
        + [dma((chips,)), dma((ax,)), dma((ay,)), dma((by,)), dma((bx,)), dma((nz - 1,))],
        compiler_params=pltpu.CompilerParams(
            collective_id=0, has_side_effects=True, vmem_limit_bytes=56 * 1024 * 1024
        ),
    )(item_table.reshape(rows // SUBLANES, SUBLANES, dim), owner_ids.T, row_ids.T, lengths[None, :], dense_input, w_bottom)
    return jnp.concatenate([pooled, dense_out], axis=1)


def solution(mesh):
    in_specs = (
        P(("row", "col"), None),
        P(("row", "col"), None),
        P(("row", "col"), None),
        P(("row", "col")),
        P(("row", "col"), None),
        P(),
    )
    out_specs = P(("row", "col"), None)
    body = functools.partial(per_device, mesh.shape["row"], mesh.shape["col"])
    return jax.shard_map(
        body, mesh=mesh, in_specs=in_specs, out_specs=out_specs, check_vma=False
    )
```

```python
import functools

import jax
import jax.numpy as jnp
from jax import lax
from jax.experimental import pallas as pl
from jax.experimental.pallas import tpu as pltpu
from jax.sharding import PartitionSpec as P

MESH = pl.DeviceIdType.MESH
LANES = 128
SUBLANES = 8


def round_up(value, unit):
    return -(-value // unit) * unit


def drain(ref, sem):
    pltpu.make_async_copy(ref, ref, sem).wait()


def kernel(
    sizes,
    table_hbm, owner_hbm, row_hbm, len_hbm, dense_hbm, w_hbm, pooled_ref, silu_ref,
    owner_ref, row_ref, len_ref, dense_ref, w_ref,
    table, owner_live, acc, index_out, index_in, index_smem, gather0, gather1,
    send_c, total, recv_c, recv_ax, recv_ay, recv_by, recv_bx, recv_z,
    owner_sem, row_sem, len_sem, dense_sem, w_sem,
    table_sem, index_send_sem, index_recv_sem, own_sem, smem_sem,
    send_c_sem, send_ax_sem, send_ay_sem, send_by_sem, send_bx_sem, send_z_sem,
    recv_c_sem, recv_ax_sem, recv_ay_sem, recv_by_sem, recv_bx_sem, recv_z_sem,
):
    nz, ncol, ny, nx, nc, cap = sizes
    owners = nz * ncol
    hist, users = owner_ref.shape
    half = users // 2
    width = acc.shape[0]
    tiles = width // LANES
    cap_rows = round_up(cap, 16)
    z = lax.axis_index("row")
    col = lax.axis_index("col")
    me = z * ncol + col
    c = col % nc
    x = (col // nc) % nx
    y = col // (nc * nx)

    def column(y_at, x_at, c_at):
        return (y_at * nx + x_at) * nc + c_at

    small = [
        pltpu.make_async_copy(*refs)
        for refs in (
            (len_hbm, len_ref, len_sem), (owner_hbm, owner_ref, owner_sem),
            (row_hbm, row_ref, row_sem), (dense_hbm, dense_ref, dense_sem),
            (w_hbm, w_ref, w_sem),
        )
    ]
    for copy in small:
        copy.start()

    pieces = 8
    piece = table.shape[0] // pieces
    for at in range(pieces):
        rows = pl.ds(at * piece, piece)
        pltpu.make_async_copy(table_hbm.at[rows], table.at[rows], table_sem).start()

    barrier = pltpu.get_barrier_semaphore()

    @pl.loop(1, owners)
    def _(step):
        there = lax.rem(me + step, owners)
        pl.semaphore_signal(
            barrier, inc=1, device_id=(there // ncol, lax.rem(there, ncol)), device_id_type=MESH
        )

    for copy in small[:3]:
        copy.wait()
    lengths = len_ref[...]
    position = lax.broadcasted_iota(jnp.int32, (hist, users), 0)
    owner_live[...] = jnp.where(position < lengths, owner_ref[...], -1)
    owner_iota = lax.broadcasted_iota(jnp.int32, (owners, users), 0)

    def count(at, carry):
        return carry + jnp.where(owner_live[pl.ds(at, 1), :] == owner_iota, 1.0, 0.0)

    per_user = lax.fori_loop(0, hist, count, jnp.zeros((owners, users), jnp.float32), unroll=5)
    before = lax.broadcasted_iota(jnp.int32, (users, users), 0) < lax.broadcasted_iota(
        jnp.int32, (users, users), 1
    )
    offsets = jnp.dot(
        per_user.astype(jnp.bfloat16),
        jnp.where(before, 1.0, 0.0).astype(jnp.bfloat16),
        preferred_element_type=jnp.float32,
    )
    acc[...] = jnp.zeros_like(acc)
    slot_iota = lax.broadcasted_iota(jnp.int32, (cap_rows, users), 0).astype(jnp.float32)
    user_number = lax.broadcasted_iota(jnp.int32, (1, users), 1).astype(jnp.float32) + 1.0
    group = 5 if hist % 5 == 0 else 1

    def place(step, counts):
        left, right = [], []
        for k in range(group):
            at = step * group + k
            row_id = row_ref[pl.ds(at, 1), :]
            high = row_id // 256
            low = (row_id - high * 256).astype(jnp.float32)
            high = high.astype(jnp.float32)
            match = owner_live[pl.ds(at, 1), :] == owner_iota
            rank = jnp.sum(jnp.where(match, counts, 0.0), axis=0, keepdims=True)
            counts = counts + jnp.where(match, 1.0, 0.0)
            right.append(jnp.where(slot_iota == rank, 1.0, 0.0).astype(jnp.bfloat16))
            values = [jnp.where(match, v, 0.0) for v in (high, low, user_number)]
            left.append(jnp.concatenate(values, axis=0).astype(jnp.bfloat16))
        acc[:cap_rows, :3 * owners] += lax.dot_general(
            jnp.concatenate(right, axis=1),
            jnp.concatenate(left, axis=1),
            (((1,), (1,)), ((), ())),
            preferred_element_type=jnp.float32,
        )
        return counts

    lax.fori_loop(0, hist // group, place, offsets)
    for at in range(tiles):
        found = acc[at * LANES:(at + 1) * LANES, :].T
        rows = found[0:owners] * 256.0 + found[owners:2 * owners]
        index_out[:, at, :] = jnp.clip(rows.astype(jnp.int32), 0, table.shape[0] - 1)
        index_out[:, tiles + at, :] = found[2 * owners:3 * owners].astype(jnp.int32)

    pl.semaphore_wait(barrier, owners - 1)

    @pl.loop(1, owners)
    def _(step):
        there = lax.rem(me + step, owners)
        pltpu.make_async_remote_copy(
            src_ref=index_out.at[there],
            dst_ref=index_in.at[me],
            send_sem=index_send_sem,
            recv_sem=index_recv_sem,
            device_id=(there // ncol, lax.rem(there, ncol)),
            device_id_type=MESH,
        ).start()

    own = pltpu.make_async_copy(index_out.at[me], index_in.at[me], own_sem)
    own.start()

    for copy in small[3:]:
        copy.wait()
    hidden = jnp.dot(dense_ref[...], w_ref[...], preferred_element_type=jnp.float32)
    dim = pooled_ref.shape[1]
    silu_ref[...] = hidden / (1.0 + jnp.exp(-hidden))
    gather0[...] = jnp.zeros_like(gather0)
    gather1[...] = jnp.zeros_like(gather1)

    own.wait()
    drain(index_in.at[pl.ds(0, owners - 1)], index_recv_sem)
    to_smem = pltpu.make_async_copy(index_in, index_smem, smem_sem)
    to_smem.start()
    to_smem.wait()
    drain(table, table_sem)

    user_iota = lax.broadcasted_iota(jnp.int32, (users, LANES), 0) + 1

    def fetch(source, gathered):
        for slot in range(cap):
            row = index_smem[source, slot // LANES, slot % LANES]
            gathered[slot:slot + 1, :] = table[pl.ds(row, 1), :]

    def block_sum(source, gathered):
        names = [index_in[source, pl.ds(tiles + at, 1), :] for at in range(tiles)]
        select = jnp.concatenate(
            [jnp.where(name == user_iota, 1.0, 0.0).astype(jnp.bfloat16) for name in names], axis=1
        )
        values = gathered[...]
        high = values.astype(jnp.bfloat16)
        low = (values - high.astype(jnp.float32)).astype(jnp.bfloat16)
        both = jnp.dot(
            select, jnp.concatenate([high, low], axis=1), preferred_element_type=jnp.float32
        )
        return both[:, :dim] + both[:, dim:]

    def send(src, dst, send_sem, recv_sem, z_at, col_at):
        pltpu.make_async_remote_copy(
            src_ref=src, dst_ref=dst, send_sem=send_sem, recv_sem=recv_sem,
            device_id=(z_at, col_at), device_id_type=MESH,
        ).start()

    def source_of(dx, dy, dz):
        return lax.rem(z + dz, nz) * ncol + column(lax.rem(y + dy, ny), lax.rem(x + dx, nx), 0)

    def offsets_at(step):
        group = step // nz
        return nx - 1 - group % nx, ny - 1 - group // nx, (step + 1) % nz

    def compute(step):
        dx, dy, dz = offsets_at(step)
        slot = (dy * nx + dx) * nz + dz
        base = source_of(dx, dy, dz)
        send_c[slot] = block_sum(base + 1 - c, gather0)
        fetch(base + c, gather1)
        send(send_c.at[slot], recv_c.at[slot], send_c_sem, recv_c_sem.at[slot],
             z, column(y, x, 1 - c))
        total[slot] = block_sum(base + c, gather1)
        fetch(source_of(*offsets_at((step + 1) % chips)) + 1 - c, gather0)

    def combine(step):
        dx, dy, dz = offsets_at(step)
        yt, xt = lax.rem(y + dy, ny), lax.rem(x + dx, nx)
        slot = (dy * nx + dx) * nz + dz
        drain(recv_c.at[slot], recv_c_sem.at[slot])
        total[slot] += recv_c[slot]
        near_x, near_y = dx == 0, dy == 0
        both = jnp.logical_and(near_x, near_y)
        upper, lower = pl.ds(0, half), pl.ds(half, half)

        def add(part, landed, sem, at):
            drain(landed.at[at], sem.at[at])
            total[slot, part] += landed[at]

        @pl.when(near_x)
        def _():
            for k in range(nx - 1):
                add(upper, recv_ax, recv_ax_sem, (k * ny + dy) * nz + dz)

        @pl.when(near_y)
        def _():
            for k in range(ny - 1):
                add(lower, recv_by, recv_by_sem, (k * nx + dx) * nz + dz)

        @pl.when(both)
        def _():
            for k in range(ny - 1):
                add(upper, recv_ay, recv_ay_sem, k * nz + dz)
            for k in range(nx - 1):
                add(lower, recv_bx, recv_bx_sem, k * nz + dz)

        @pl.when(dx > 0)
        def _():
            at = ((dx - 1) * ny + dy) * nz + dz
            send(total.at[slot, upper], recv_ax.at[at], send_ax_sem, recv_ax_sem.at[at],
                 z, column(y, xt, c))

        @pl.when(dy > 0)
        def _():
            at = ((dy - 1) * nx + dx) * nz + dz
            send(total.at[slot, lower], recv_by.at[at], send_by_sem, recv_by_sem.at[at],
                 z, column(yt, x, c))

        @pl.when(jnp.logical_and(near_x, dy > 0))
        def _():
            at = (dy - 1) * nz + dz
            send(total.at[slot, upper], recv_ay.at[at], send_ay_sem, recv_ay_sem.at[at],
                 z, column(yt, x, c))

        @pl.when(jnp.logical_and(near_y, dx > 0))
        def _():
            at = (dx - 1) * nz + dz
            send(total.at[slot, lower], recv_bx.at[at], send_bx_sem, recv_bx_sem.at[at],
                 z, column(y, xt, c))

        @pl.when(jnp.logical_and(both, dz > 0))
        def _():
            send(total.at[dz], recv_z.at[dz - 1], send_z_sem, recv_z_sem.at[dz - 1],
                 lax.rem(z + dz, nz), col)

    chips = nz * ny * nx
    fetch(source_of(*offsets_at(0)) + 1 - c, gather0)

    delay = min(3, chips)

    @pl.loop(0, chips + delay)
    def _(step):
        @pl.when(step < chips)
        def _():
            compute(step)

        @pl.when(step >= delay)
        def _():
            combine(step - delay)

    pooled = total[0]
    for k in range(nz - 1):
        drain(recv_z.at[k], recv_z_sem.at[k])
        pooled = pooled + recv_z[k]
    divisor = jnp.broadcast_to(lengths.astype(jnp.float32), (users, users)).T
    pooled_ref[...] = pooled / divisor[:, :1]

    drain(index_in.at[pl.ds(0, owners - 1)], index_send_sem)
    drain(send_c, send_c_sem)
    drain(recv_ax, send_ax_sem)
    drain(recv_ay, send_ay_sem)
    drain(recv_by, send_by_sem)
    drain(recv_bx, send_bx_sem)
    drain(recv_z, send_z_sem)


def per_device(nz, ncol, item_table, owner_ids, row_ids, lengths, dense_input, w_bottom):
    users, hist = owner_ids.shape
    rows, dim = item_table.shape
    owners = nz * ncol
    cap = 3 * users * hist // (2 * owners)
    width = round_up(cap, LANES)
    tile_rows = round_up(2 * (width // LANES), SUBLANES)
    nc, nx = 2, 2
    ny = ncol // (nc * nx)
    chips = nz * ny * nx
    half = users // 2
    ax, ay, by, bx = (nx - 1) * ny * nz, (ny - 1) * nz, (ny - 1) * nx * nz, (nx - 1) * nz
    dma = pltpu.SemaphoreType.DMA
    vmem = pl.BlockSpec(memory_space=pltpu.VMEM)

    def floats(*shape):
        return pltpu.VMEM(shape, jnp.float32)

    pooled, dense_out = pl.pallas_call(
        functools.partial(kernel, (nz, ncol, ny, nx, nc, cap)),
        out_shape=[
            jax.ShapeDtypeStruct((users, dim), jnp.float32),
            jax.ShapeDtypeStruct((users, w_bottom.shape[1]), jnp.float32),
        ],
        in_specs=[pl.BlockSpec(memory_space=pl.ANY)] * 6,
        out_specs=[vmem, vmem],
        scratch_shapes=[
            pltpu.VMEM((hist, users), jnp.int32),
            pltpu.VMEM((hist, users), jnp.int32),
            pltpu.VMEM((1, users), jnp.int32),
            pltpu.VMEM(dense_input.shape, dense_input.dtype),
            pltpu.VMEM(w_bottom.shape, w_bottom.dtype),
            floats(rows, dim),
            pltpu.VMEM((hist, users), jnp.int32),
            floats(width, round_up(3 * owners, LANES)),
            pltpu.VMEM((owners, tile_rows, LANES), jnp.int32),
            pltpu.VMEM((owners, tile_rows, LANES), jnp.int32),
            pltpu.SMEM((owners, tile_rows, LANES), jnp.int32),
            floats(width, dim),
            floats(width, dim),
            floats(chips, users, dim),
            floats(chips, users, dim),
            floats(chips, users, dim),
            floats(ax, half, dim),
            floats(ay, half, dim),
            floats(by, half, dim),
            floats(bx, half, dim),
            floats(nz - 1, users, dim),
        ]
        + [dma] * 16
        + [dma((chips,)), dma((ax,)), dma((ay,)), dma((by,)), dma((bx,)), dma((nz - 1,))],
        compiler_params=pltpu.CompilerParams(
            collective_id=0, has_side_effects=True, vmem_limit_bytes=56 * 1024 * 1024
        ),
    )(item_table, owner_ids.T, row_ids.T, lengths[None, :], dense_input, w_bottom)
    return jnp.concatenate([pooled, dense_out], axis=1)


def solution(mesh):
    in_specs = (
        P(("row", "col"), None),
        P(("row", "col"), None),
        P(("row", "col"), None),
        P(("row", "col")),
        P(("row", "col"), None),
        P(),
    )
    out_specs = P(("row", "col"), None)
    body = functools.partial(per_device, mesh.shape["row"], mesh.shape["col"])
    return jax.shard_map(
        body, mesh=mesh, in_specs=in_specs, out_specs=out_specs, check_vma=False
    )
```

```python
import functools

import jax
import jax.numpy as jnp
from jax import lax
from jax.experimental import pallas as pl
from jax.experimental.pallas import tpu as pltpu
from jax.sharding import PartitionSpec as P

MESH = pl.DeviceIdType.MESH
LANES = 128
SUBLANES = 8


def round_up(value, unit):
    return -(-value // unit) * unit


def drain(ref, sem):
    pltpu.make_async_copy(ref, ref, sem).wait()


def kernel(
    sizes,
    table_hbm, owner_hbm, row_hbm, len_hbm, dense_hbm, w_hbm, pooled_ref, silu_ref,
    owner_ref, row_ref, len_ref, dense_ref, w_ref,
    table, owner_live, acc, index_out, index_in, index_smem, gather0, gather1,
    send_c, total, recv_c, recv_ax, recv_ay, recv_by, recv_bx, recv_z,
    owner_sem, row_sem, len_sem, dense_sem, w_sem,
    table_sem, index_send_sem, index_recv_sem, own_sem,
    send_c_sem, send_ax_sem, send_ay_sem, send_by_sem, send_bx_sem, send_z_sem, smem_sem,
    recv_c_sem, recv_ax_sem, recv_ay_sem, recv_by_sem, recv_bx_sem, recv_z_sem,
):
    nz, ncol, ny, nx, nc, cap = sizes
    owners = nz * ncol
    hist, users = owner_ref.shape
    half = users // 2
    width = acc.shape[0]
    tiles = width // LANES
    cap_rows = round_up(cap, 16)
    z = lax.axis_index("row")
    col = lax.axis_index("col")
    me = z * ncol + col
    c = col % nc
    x = (col // nc) % nx
    y = col // (nc * nx)

    def column(y_at, x_at, c_at):
        return (y_at * nx + x_at) * nc + c_at

    small = [
        pltpu.make_async_copy(*refs)
        for refs in (
            (len_hbm, len_ref, len_sem), (owner_hbm, owner_ref, owner_sem),
            (row_hbm, row_ref, row_sem), (dense_hbm, dense_ref, dense_sem),
            (w_hbm, w_ref, w_sem),
        )
    ]
    for copy in small:
        copy.start()

    pieces = 8
    piece = table.shape[0] // pieces
    for at in range(pieces):
        rows = pl.ds(at * piece, piece)
        pltpu.make_async_copy(table_hbm.at[rows], table.at[rows], table_sem).start()

    barrier = pltpu.get_barrier_semaphore()

    @pl.loop(1, owners)
    def _(step):
        there = lax.rem(me + step, owners)
        pl.semaphore_signal(
            barrier, inc=1, device_id=(there // ncol, lax.rem(there, ncol)), device_id_type=MESH
        )

    for copy in small[:3]:
        copy.wait()
    lengths = len_ref[...]
    position = lax.broadcasted_iota(jnp.int32, (hist, users), 0)
    owner_live[...] = jnp.where(position < lengths, owner_ref[...], -1)
    owner_iota = lax.broadcasted_iota(jnp.int32, (owners, users), 0)

    def count(at, carry):
        return carry + jnp.where(owner_live[pl.ds(at, 1), :] == owner_iota, 1.0, 0.0)

    per_user = lax.fori_loop(0, hist, count, jnp.zeros((owners, users), jnp.float32), unroll=5)
    before = lax.broadcasted_iota(jnp.int32, (users, users), 0) < lax.broadcasted_iota(
        jnp.int32, (users, users), 1
    )
    offsets = jnp.dot(
        per_user.astype(jnp.bfloat16),
        jnp.where(before, 1.0, 0.0).astype(jnp.bfloat16),
        preferred_element_type=jnp.float32,
    )
    acc[...] = jnp.zeros_like(acc)
    slot_iota = lax.broadcasted_iota(jnp.int32, (cap_rows, users), 0).astype(jnp.float32)
    user_number = lax.broadcasted_iota(jnp.int32, (1, users), 1).astype(jnp.float32) + 1.0
    group = 5 if hist % 5 == 0 else 1

    def place(step, counts):
        left, right = [], []
        for k in range(group):
            at = step * group + k
            row_id = row_ref[pl.ds(at, 1), :]
            high = row_id // 256
            low = (row_id - high * 256).astype(jnp.float32)
            high = high.astype(jnp.float32)
            match = owner_live[pl.ds(at, 1), :] == owner_iota
            rank = jnp.sum(jnp.where(match, counts, 0.0), axis=0, keepdims=True)
            counts = counts + jnp.where(match, 1.0, 0.0)
            right.append(jnp.where(slot_iota == rank, 1.0, 0.0).astype(jnp.bfloat16))
            values = [jnp.where(match, v, 0.0) for v in (high, low, user_number)]
            left.append(jnp.concatenate(values, axis=0).astype(jnp.bfloat16))
        acc[:cap_rows, :3 * owners] += lax.dot_general(
            jnp.concatenate(right, axis=1),
            jnp.concatenate(left, axis=1),
            (((1,), (1,)), ((), ())),
            preferred_element_type=jnp.float32,
        )
        return counts

    lax.fori_loop(0, hist // group, place, offsets)
    for at in range(tiles):
        found = acc[at * LANES:(at + 1) * LANES, :].T
        rows = found[0:owners] * 256.0 + found[owners:2 * owners]
        index_out[:, at, :] = jnp.clip(rows.astype(jnp.int32), 0, table.shape[0] - 1)
        index_out[:, tiles + at, :] = found[2 * owners:3 * owners].astype(jnp.int32)

    pl.semaphore_wait(barrier, owners - 1)

    @pl.loop(1, owners)
    def _(step):
        there = lax.rem(me + step, owners)
        pltpu.make_async_remote_copy(
            src_ref=index_out.at[there],
            dst_ref=index_in.at[me],
            send_sem=index_send_sem,
            recv_sem=index_recv_sem,
            device_id=(there // ncol, lax.rem(there, ncol)),
            device_id_type=MESH,
        ).start()

    own = pltpu.make_async_copy(index_out.at[me], index_in.at[me], own_sem)
    own.start()

    for copy in small[3:]:
        copy.wait()
    hidden = jnp.dot(dense_ref[...], w_ref[...], preferred_element_type=jnp.float32)
    dim = pooled_ref.shape[1]
    silu_ref[...] = hidden / (1.0 + jnp.exp(-hidden))
    gather0[...] = jnp.zeros_like(gather0)
    gather1[...] = jnp.zeros_like(gather1)

    own.wait()
    drain(index_in.at[pl.ds(0, owners - 1)], index_recv_sem)
    chips = nz * ny * nx

    def offsets_at(step):
        group = step % (nx * ny)
        return nx - 1 - group % nx, ny - 1 - group // nx, (step // (nx * ny) + 1) % nz

    def source_of(dx, dy, dz):
        return lax.rem(z + dz, nz) * ncol + column(lax.rem(y + dy, ny), lax.rem(x + dx, nx), 0)

    def to_smem(source):
        return pltpu.make_async_copy(
            index_in.at[source], index_smem.at[source], smem_sem.at[source]
        )

    @pl.loop(0, chips)
    def _(step):
        base = source_of(*offsets_at(step))
        to_smem(base + 1 - c).start()
        to_smem(base + c).start()

    drain(table, table_sem)

    user_iota = lax.broadcasted_iota(jnp.int32, (users, LANES), 0) + 1

    def fetch(source, gathered):
        for slot in range(cap):
            row = index_smem[source, slot // LANES, slot % LANES]
            gathered[slot:slot + 1, :] = table[pl.ds(row, 1), :]

    def block_sum(source, gathered):
        names = [index_in[source, pl.ds(tiles + at, 1), :] for at in range(tiles)]
        select = jnp.concatenate(
            [jnp.where(name == user_iota, 1.0, 0.0).astype(jnp.bfloat16) for name in names], axis=1
        )
        values = gathered[...]
        high = values.astype(jnp.bfloat16)
        low = (values - high.astype(jnp.float32)).astype(jnp.bfloat16)
        both = jnp.dot(
            select, jnp.concatenate([high, low], axis=1), preferred_element_type=jnp.float32
        )
        return both[:, :dim] + both[:, dim:]

    def send(src, dst, send_sem, recv_sem, z_at, col_at):
        pltpu.make_async_remote_copy(
            src_ref=src, dst_ref=dst, send_sem=send_sem, recv_sem=recv_sem,
            device_id=(z_at, col_at), device_id_type=MESH,
        ).start()

    def compute(step):
        dx, dy, dz = offsets_at(step)
        slot = (dy * nx + dx) * nz + dz
        base = source_of(dx, dy, dz)
        following = source_of(*offsets_at((step + 1) % chips))
        to_smem(base + c).wait()

        @pl.when(step + 1 < chips)
        def _():
            to_smem(following + 1 - c).wait()

        send_c[slot] = block_sum(base + 1 - c, gather0)
        fetch(base + c, gather1)
        send(send_c.at[slot], recv_c.at[slot], send_c_sem, recv_c_sem.at[slot],
             z, column(y, x, 1 - c))
        total[slot] = block_sum(base + c, gather1)
        fetch(following + 1 - c, gather0)

    upper, lower = pl.ds(0, half), pl.ds(half, half)

    def add(slot, part, landed, sem, at):
        drain(landed.at[at], sem.at[at])
        total[slot, part] += landed[at]

    def after_core(step):
        dx, dy, dz = offsets_at(step)
        slot = (dy * nx + dx) * nz + dz
        drain(recv_c.at[slot], recv_c_sem.at[slot])
        total[slot] += recv_c[slot]

        @pl.when(dx > 0)
        def _():
            at = ((dx - 1) * ny + dy) * nz + dz
            send(total.at[slot, upper], recv_ax.at[at], send_ax_sem, recv_ax_sem.at[at],
                 z, column(y, lax.rem(x + dx, nx), c))

        @pl.when(dy > 0)
        def _():
            at = ((dy - 1) * nx + dx) * nz + dz
            send(total.at[slot, lower], recv_by.at[at], send_by_sem, recv_by_sem.at[at],
                 z, column(lax.rem(y + dy, ny), x, c))

    def after_first(step):
        dx, dy, dz = offsets_at(step)
        slot = (dy * nx + dx) * nz + dz

        @pl.when(dx == 0)
        def _():
            for k in range(nx - 1):
                add(slot, upper, recv_ax, recv_ax_sem, (k * ny + dy) * nz + dz)

        @pl.when(dy == 0)
        def _():
            for k in range(ny - 1):
                add(slot, lower, recv_by, recv_by_sem, (k * nx + dx) * nz + dz)

        @pl.when(jnp.logical_and(dx == 0, dy > 0))
        def _():
            at = (dy - 1) * nz + dz
            send(total.at[slot, upper], recv_ay.at[at], send_ay_sem, recv_ay_sem.at[at],
                 z, column(lax.rem(y + dy, ny), x, c))

        @pl.when(jnp.logical_and(dy == 0, dx > 0))
        def _():
            at = (dx - 1) * nz + dz
            send(total.at[slot, lower], recv_bx.at[at], send_bx_sem, recv_bx_sem.at[at],
                 z, column(y, lax.rem(x + dx, nx), c))

    def after_second(step):
        dx, dy, dz = offsets_at(step)

        @pl.when(jnp.logical_and(dx == 0, dy == 0))
        def _():
            for k in range(ny - 1):
                add(dz, upper, recv_ay, recv_ay_sem, k * nz + dz)
            for k in range(nx - 1):
                add(dz, lower, recv_bx, recv_bx_sem, k * nz + dz)

            @pl.when(dz > 0)
            def _():
                send(total.at[dz], recv_z.at[dz - 1], send_z_sem, recv_z_sem.at[dz - 1],
                     lax.rem(z + dz, nz), col)

    first_source = source_of(*offsets_at(0)) + 1 - c
    to_smem(first_source).wait()
    fetch(first_source, gather0)
    delays = (2, 4, 6)

    @pl.loop(0, chips + delays[-1])
    def _(step):
        @pl.when(step < chips)
        def _():
            compute(step)

        for delay, stage in zip(delays, (after_core, after_first, after_second)):

            @pl.when(jnp.logical_and(step >= delay, step < chips + delay))
            def _():
                stage(step - delay)

    pooled = total[0]
    for k in range(nz - 1):
        drain(recv_z.at[k], recv_z_sem.at[k])
        pooled = pooled + recv_z[k]
    divisor = jnp.broadcast_to(lengths.astype(jnp.float32), (users, users)).T
    pooled_ref[...] = pooled / divisor[:, :1]

    drain(index_in.at[pl.ds(0, owners - 1)], index_send_sem)
    drain(send_c, send_c_sem)
    drain(recv_ax, send_ax_sem)
    drain(recv_ay, send_ay_sem)
    drain(recv_by, send_by_sem)
    drain(recv_bx, send_bx_sem)
    drain(recv_z, send_z_sem)


def per_device(nz, ncol, item_table, owner_ids, row_ids, lengths, dense_input, w_bottom):
    users, hist = owner_ids.shape
    rows, dim = item_table.shape
    owners = nz * ncol
    cap = 3 * users * hist // (2 * owners)
    width = round_up(cap, LANES)
    tile_rows = round_up(2 * (width // LANES), SUBLANES)
    nc, nx = 2, 2
    ny = ncol // (nc * nx)
    chips = nz * ny * nx
    half = users // 2
    ax, ay, by, bx = (nx - 1) * ny * nz, (ny - 1) * nz, (ny - 1) * nx * nz, (nx - 1) * nz
    dma = pltpu.SemaphoreType.DMA
    vmem = pl.BlockSpec(memory_space=pltpu.VMEM)

    def floats(*shape):
        return pltpu.VMEM(shape, jnp.float32)

    pooled, dense_out = pl.pallas_call(
        functools.partial(kernel, (nz, ncol, ny, nx, nc, cap)),
        out_shape=[
            jax.ShapeDtypeStruct((users, dim), jnp.float32),
            jax.ShapeDtypeStruct((users, w_bottom.shape[1]), jnp.float32),
        ],
        in_specs=[pl.BlockSpec(memory_space=pl.ANY)] * 6,
        out_specs=[vmem, vmem],
        scratch_shapes=[
            pltpu.VMEM((hist, users), jnp.int32),
            pltpu.VMEM((hist, users), jnp.int32),
            pltpu.VMEM((1, users), jnp.int32),
            pltpu.VMEM(dense_input.shape, dense_input.dtype),
            pltpu.VMEM(w_bottom.shape, w_bottom.dtype),
            floats(rows, dim),
            pltpu.VMEM((hist, users), jnp.int32),
            floats(width, round_up(3 * owners, LANES)),
            pltpu.VMEM((owners, tile_rows, LANES), jnp.int32),
            pltpu.VMEM((owners, tile_rows, LANES), jnp.int32),
            pltpu.SMEM((owners, tile_rows, LANES), jnp.int32),
            floats(width, dim),
            floats(width, dim),
            floats(chips, users, dim),
            floats(chips, users, dim),
            floats(chips, users, dim),
            floats(ax, half, dim),
            floats(ay, half, dim),
            floats(by, half, dim),
            floats(bx, half, dim),
            floats(nz - 1, users, dim),
        ]
        + [dma] * 15 + [dma((owners,))]
        + [dma((chips,)), dma((ax,)), dma((ay,)), dma((by,)), dma((bx,)), dma((nz - 1,))],
        compiler_params=pltpu.CompilerParams(
            collective_id=0, has_side_effects=True, vmem_limit_bytes=56 * 1024 * 1024
        ),
    )(item_table, owner_ids.T, row_ids.T, lengths[None, :], dense_input, w_bottom)
    return jnp.concatenate([pooled, dense_out], axis=1)


def solution(mesh):
    in_specs = (
        P(("row", "col"), None),
        P(("row", "col"), None),
        P(("row", "col"), None),
        P(("row", "col")),
        P(("row", "col"), None),
        P(),
    )
    out_specs = P(("row", "col"), None)
    body = functools.partial(per_device, mesh.shape["row"], mesh.shape["col"])
    return jax.shard_map(
        body, mesh=mesh, in_specs=in_specs, out_specs=out_specs, check_vma=False
    )
```

```python
import functools

import jax
import jax.numpy as jnp
from jax import lax
from jax.experimental import pallas as pl
from jax.experimental.pallas import tpu as pltpu
from jax.sharding import PartitionSpec as P

MESH = pl.DeviceIdType.MESH
LANES = 128
SUBLANES = 8


def round_up(value, unit):
    return -(-value // unit) * unit


def quotient(value, unit):
    if unit & (unit - 1) == 0:
        return value >> (unit.bit_length() - 1)
    return value // unit


def remainder(value, unit):
    if unit & (unit - 1) == 0:
        return value & (unit - 1)
    return value % unit


def drain(ref, sem):
    pltpu.make_async_copy(ref, ref, sem).wait()


def kernel(
    sizes,
    table_hbm, owner_hbm, row_hbm, len_hbm, dense_hbm, w_hbm, pooled_ref, silu_ref,
    owner_ref, row_ref, len_ref, dense_ref, w_ref,
    table, owner_live, acc, index_out, index_in, index_smem, gather0, gather1,
    send_c, total, recv_c, recv_ax, recv_ay, recv_by, recv_bx, recv_z,
    owner_sem, row_sem, len_sem, dense_sem, w_sem,
    table_sem, index_send_sem, index_recv_sem, own_sem,
    send_c_sem, send_ax_sem, send_ay_sem, send_by_sem, send_bx_sem, send_z_sem, smem_sem,
    recv_c_sem, recv_ax_sem, recv_ay_sem, recv_by_sem, recv_bx_sem, recv_z_sem,
):
    nz, ncol, ny, nx, nc, cap = sizes
    owners = nz * ncol
    hist, users = owner_ref.shape
    half = users // 2
    width = acc.shape[0]
    tiles = width // LANES
    cap_rows = round_up(cap, 16)
    z = lax.axis_index("row")
    col = lax.axis_index("col")
    me = z * ncol + col
    c = remainder(col, nc)
    x = remainder(quotient(col, nc), nx)
    y = quotient(col, nc * nx)

    def column(y_at, x_at, c_at):
        return (y_at * nx + x_at) * nc + c_at

    small = [
        pltpu.make_async_copy(*refs)
        for refs in (
            (len_hbm, len_ref, len_sem), (owner_hbm, owner_ref, owner_sem),
            (row_hbm, row_ref, row_sem), (dense_hbm, dense_ref, dense_sem),
            (w_hbm, w_ref, w_sem),
        )
    ]
    for copy in small:
        copy.start()

    pieces = 32
    piece = table.shape[0] // pieces
    for at in range(pieces):
        rows = pl.ds(at * piece, piece)
        pltpu.make_async_copy(table_hbm.at[rows], table.at[rows], table_sem).start()

    barrier = pltpu.get_barrier_semaphore()

    @pl.loop(1, owners)
    def _(step):
        there = remainder(me + step, owners)
        pl.semaphore_signal(
            barrier, inc=1, device_id=(quotient(there, ncol), remainder(there, ncol)), device_id_type=MESH
        )

    for copy in small[:3]:
        copy.wait()
    lengths = len_ref[...]
    position = lax.broadcasted_iota(jnp.int32, (hist, users), 0)
    owner_live[...] = jnp.where(position < lengths, owner_ref[...], -1)
    owner_iota = lax.broadcasted_iota(jnp.int32, (owners, users), 0)

    def count(at, carry):
        return carry + jnp.where(owner_live[pl.ds(at, 1), :] == owner_iota, 1.0, 0.0)

    per_user = lax.fori_loop(0, hist, count, jnp.zeros((owners, users), jnp.float32), unroll=5)
    before = lax.broadcasted_iota(jnp.int32, (users, users), 0) < lax.broadcasted_iota(
        jnp.int32, (users, users), 1
    )
    offsets = jnp.dot(
        per_user.astype(jnp.bfloat16),
        jnp.where(before, 1.0, 0.0).astype(jnp.bfloat16),
        preferred_element_type=jnp.float32,
    )
    acc[...] = jnp.zeros_like(acc)
    slot_iota = lax.broadcasted_iota(jnp.int32, (cap_rows, users), 0).astype(jnp.float32)
    user_number = lax.broadcasted_iota(jnp.int32, (1, users), 1).astype(jnp.float32) + 1.0
    group = 5 if hist % 5 == 0 else 1

    def place(step, counts):
        left, right = [], []
        for k in range(group):
            at = step * group + k
            row_id = row_ref[pl.ds(at, 1), :]
            high = row_id >> 8
            low = (row_id & 255).astype(jnp.float32)
            high = high.astype(jnp.float32)
            match = owner_live[pl.ds(at, 1), :] == owner_iota
            rank = jnp.sum(jnp.where(match, counts, 0.0), axis=0, keepdims=True)
            counts = counts + jnp.where(match, 1.0, 0.0)
            right.append(jnp.where(slot_iota == rank, 1.0, 0.0).astype(jnp.bfloat16))
            values = [jnp.where(match, v, 0.0) for v in (high, low, user_number)]
            left.append(jnp.concatenate(values, axis=0).astype(jnp.bfloat16))
        acc[:cap_rows, :3 * owners] += lax.dot_general(
            jnp.concatenate(right, axis=1),
            jnp.concatenate(left, axis=1),
            (((1,), (1,)), ((), ())),
            preferred_element_type=jnp.float32,
        )
        return counts

    lax.fori_loop(0, hist // group, place, offsets)
    for at in range(tiles):
        found = acc[at * LANES:(at + 1) * LANES, :].T
        rows = found[0:owners] * 256.0 + found[owners:2 * owners]
        index_out[:, at, :] = jnp.clip(rows.astype(jnp.int32), 0, table.shape[0] - 1)
        index_out[:, tiles + at, :] = found[2 * owners:3 * owners].astype(jnp.int32)

    pl.semaphore_wait(barrier, owners - 1)

    @pl.loop(1, owners)
    def _(step):
        there = remainder(me + step, owners)
        pltpu.make_async_remote_copy(
            src_ref=index_out.at[there],
            dst_ref=index_in.at[me],
            send_sem=index_send_sem,
            recv_sem=index_recv_sem,
            device_id=(quotient(there, ncol), remainder(there, ncol)),
            device_id_type=MESH,
        ).start()

    own = pltpu.make_async_copy(index_out.at[me], index_in.at[me], own_sem)
    own.start()

    for copy in small[3:]:
        copy.wait()
    hidden = jnp.dot(dense_ref[...], w_ref[...], preferred_element_type=jnp.float32)
    dim = pooled_ref.shape[1]
    silu_ref[...] = hidden / (1.0 + jnp.exp(-hidden))
    gather0[...] = jnp.zeros_like(gather0)
    gather1[...] = jnp.zeros_like(gather1)

    own.wait()
    drain(index_in.at[pl.ds(0, owners - 1)], index_recv_sem)
    chips = nz * ny * nx

    def offsets_at(step):
        group = remainder(step, nx * ny)
        return (
            nx - 1 - remainder(group, nx),
            ny - 1 - quotient(group, nx),
            remainder(quotient(step, nx * ny) + 1, nz),
        )

    def source_of(dx, dy, dz):
        return remainder(z + dz, nz) * ncol + column(remainder(y + dy, ny), remainder(x + dx, nx), 0)

    def to_smem(source):
        return pltpu.make_async_copy(
            index_in.at[source], index_smem.at[source], smem_sem.at[source]
        )

    @pl.loop(0, chips)
    def _(step):
        base = source_of(*offsets_at(step))
        to_smem(base + 1 - c).start()
        to_smem(base + c).start()

    drain(table, table_sem)

    user_iota = lax.broadcasted_iota(jnp.int32, (users, LANES), 0) + 1

    def fetch(source, gathered):
        for slot in range(cap):
            row = index_smem[source, slot // LANES, slot % LANES]
            gathered[slot:slot + 1, :] = table[pl.ds(row, 1), :]

    def block_sum(source, gathered):
        names = [index_in[source, pl.ds(tiles + at, 1), :] for at in range(tiles)]
        select = jnp.concatenate(
            [jnp.where(name == user_iota, 1.0, 0.0).astype(jnp.bfloat16) for name in names], axis=1
        )
        values = gathered[...]
        high = values.astype(jnp.bfloat16)
        low = (values - high.astype(jnp.float32)).astype(jnp.bfloat16)
        both = jnp.dot(
            select, jnp.concatenate([high, low], axis=1), preferred_element_type=jnp.float32
        )
        return both[:, :dim] + both[:, dim:]

    def send(src, dst, send_sem, recv_sem, z_at, col_at):
        pltpu.make_async_remote_copy(
            src_ref=src, dst_ref=dst, send_sem=send_sem, recv_sem=recv_sem,
            device_id=(z_at, col_at), device_id_type=MESH,
        ).start()

    def compute(step):
        dx, dy, dz = offsets_at(step)
        slot = (dy * nx + dx) * nz + dz
        base = source_of(dx, dy, dz)
        following = source_of(*offsets_at(remainder(step + 1, chips)))
        to_smem(base + c).wait()

        @pl.when(step + 1 < chips)
        def _():
            to_smem(following + 1 - c).wait()

        send_c[slot] = block_sum(base + 1 - c, gather0)
        fetch(base + c, gather1)
        send(send_c.at[slot], recv_c.at[slot], send_c_sem, recv_c_sem.at[slot],
             z, column(y, x, 1 - c))
        total[slot] = block_sum(base + c, gather1)
        fetch(following + 1 - c, gather0)

    upper, lower = pl.ds(0, half), pl.ds(half, half)

    def add(slot, part, landed, sem, at):
        drain(landed.at[at], sem.at[at])
        total[slot, part] += landed[at]

    def after_core(step):
        dx, dy, dz = offsets_at(step)
        slot = (dy * nx + dx) * nz + dz
        drain(recv_c.at[slot], recv_c_sem.at[slot])
        total[slot] += recv_c[slot]

        @pl.when(dx > 0)
        def _():
            at = ((dx - 1) * ny + dy) * nz + dz
            send(total.at[slot, upper], recv_ax.at[at], send_ax_sem, recv_ax_sem.at[at],
                 z, column(y, remainder(x + dx, nx), c))

        @pl.when(dy > 0)
        def _():
            at = ((dy - 1) * nx + dx) * nz + dz
            send(total.at[slot, lower], recv_by.at[at], send_by_sem, recv_by_sem.at[at],
                 z, column(remainder(y + dy, ny), x, c))

    def after_first(step):
        dx, dy, dz = offsets_at(step)
        slot = (dy * nx + dx) * nz + dz

        @pl.when(dx == 0)
        def _():
            for k in range(nx - 1):
                add(slot, upper, recv_ax, recv_ax_sem, (k * ny + dy) * nz + dz)

        @pl.when(dy == 0)
        def _():
            for k in range(ny - 1):
                add(slot, lower, recv_by, recv_by_sem, (k * nx + dx) * nz + dz)

        @pl.when(jnp.logical_and(dx == 0, dy > 0))
        def _():
            at = (dy - 1) * nz + dz
            send(total.at[slot, upper], recv_ay.at[at], send_ay_sem, recv_ay_sem.at[at],
                 z, column(remainder(y + dy, ny), x, c))

        @pl.when(jnp.logical_and(dy == 0, dx > 0))
        def _():
            at = (dx - 1) * nz + dz
            send(total.at[slot, lower], recv_bx.at[at], send_bx_sem, recv_bx_sem.at[at],
                 z, column(y, remainder(x + dx, nx), c))

    def after_second(step):
        dx, dy, dz = offsets_at(step)

        @pl.when(jnp.logical_and(dx == 0, dy == 0))
        def _():
            for k in range(ny - 1):
                add(dz, upper, recv_ay, recv_ay_sem, k * nz + dz)
            for k in range(nx - 1):
                add(dz, lower, recv_bx, recv_bx_sem, k * nz + dz)

            @pl.when(dz > 0)
            def _():
                send(total.at[dz], recv_z.at[dz - 1], send_z_sem, recv_z_sem.at[dz - 1],
                     remainder(z + dz, nz), col)

    first_source = source_of(*offsets_at(0)) + 1 - c
    to_smem(first_source).wait()
    fetch(first_source, gather0)
    delays = (2, 4, 6)

    @pl.loop(0, chips + delays[-1])
    def _(step):
        @pl.when(step < chips)
        def _():
            compute(step)

        for delay, stage in zip(delays, (after_core, after_first, after_second)):

            @pl.when(jnp.logical_and(step >= delay, step < chips + delay))
            def _():
                stage(step - delay)

    pooled = total[0]
    for k in range(nz - 1):
        drain(recv_z.at[k], recv_z_sem.at[k])
        pooled = pooled + recv_z[k]
    divisor = jnp.broadcast_to(lengths.astype(jnp.float32), (users, users)).T
    pooled_ref[...] = pooled / divisor[:, :1]

    drain(index_in.at[pl.ds(0, owners - 1)], index_send_sem)
    drain(send_c, send_c_sem)
    drain(recv_ax, send_ax_sem)
    drain(recv_ay, send_ay_sem)
    drain(recv_by, send_by_sem)
    drain(recv_bx, send_bx_sem)
    drain(recv_z, send_z_sem)


def per_device(nz, ncol, item_table, owner_ids, row_ids, lengths, dense_input, w_bottom):
    users, hist = owner_ids.shape
    rows, dim = item_table.shape
    owners = nz * ncol
    cap = 3 * users * hist // (2 * owners)
    width = round_up(cap, LANES)
    tile_rows = round_up(2 * (width // LANES), SUBLANES)
    nc, nx = 2, 2
    ny = ncol // (nc * nx)
    chips = nz * ny * nx
    half = users // 2
    ax, ay, by, bx = (nx - 1) * ny * nz, (ny - 1) * nz, (ny - 1) * nx * nz, (nx - 1) * nz
    dma = pltpu.SemaphoreType.DMA
    vmem = pl.BlockSpec(memory_space=pltpu.VMEM)

    def floats(*shape):
        return pltpu.VMEM(shape, jnp.float32)

    pooled, dense_out = pl.pallas_call(
        functools.partial(kernel, (nz, ncol, ny, nx, nc, cap)),
        out_shape=[
            jax.ShapeDtypeStruct((users, dim), jnp.float32),
            jax.ShapeDtypeStruct((users, w_bottom.shape[1]), jnp.float32),
        ],
        in_specs=[pl.BlockSpec(memory_space=pl.ANY)] * 6,
        out_specs=[vmem, vmem],
        scratch_shapes=[
            pltpu.VMEM((hist, users), jnp.int32),
            pltpu.VMEM((hist, users), jnp.int32),
            pltpu.VMEM((1, users), jnp.int32),
            pltpu.VMEM(dense_input.shape, dense_input.dtype),
            pltpu.VMEM(w_bottom.shape, w_bottom.dtype),
            floats(rows, dim),
            pltpu.VMEM((hist, users), jnp.int32),
            floats(width, round_up(3 * owners, LANES)),
            pltpu.VMEM((owners, tile_rows, LANES), jnp.int32),
            pltpu.VMEM((owners, tile_rows, LANES), jnp.int32),
            pltpu.SMEM((owners, tile_rows, LANES), jnp.int32),
            floats(width, dim),
            floats(width, dim),
            floats(chips, users, dim),
            floats(chips, users, dim),
            floats(chips, users, dim),
            floats(ax, half, dim),
            floats(ay, half, dim),
            floats(by, half, dim),
            floats(bx, half, dim),
            floats(nz - 1, users, dim),
        ]
        + [dma] * 15 + [dma((owners,))]
        + [dma((chips,)), dma((ax,)), dma((ay,)), dma((by,)), dma((bx,)), dma((nz - 1,))],
        compiler_params=pltpu.CompilerParams(
            collective_id=0, has_side_effects=True, vmem_limit_bytes=56 * 1024 * 1024
        ),
    )(item_table, owner_ids.T, row_ids.T, lengths[None, :], dense_input, w_bottom)
    return jnp.concatenate([pooled, dense_out], axis=1)


def solution(mesh):
    in_specs = (
        P(("row", "col"), None),
        P(("row", "col"), None),
        P(("row", "col"), None),
        P(("row", "col")),
        P(("row", "col"), None),
        P(),
    )
    out_specs = P(("row", "col"), None)
    body = functools.partial(per_device, mesh.shape["row"], mesh.shape["col"])
    return jax.shard_map(
        body, mesh=mesh, in_specs=in_specs, out_specs=out_specs, check_vma=False
    )
```

```python
import functools

import jax
import jax.numpy as jnp
from jax import lax
from jax.experimental import pallas as pl
from jax.experimental.pallas import tpu as pltpu
from jax.sharding import PartitionSpec as P

MESH = pl.DeviceIdType.MESH
LANES = 128
SUBLANES = 8


def round_up(value, unit):
    return -(-value // unit) * unit


def drain(ref, sem):
    pltpu.make_async_copy(ref, ref, sem).wait()


def kernel(
    sizes,
    table_hbm, owner_hbm, row_hbm, len_hbm, dense_hbm, w_hbm, pooled_ref, silu_ref,
    owner_ref, row_ref, len_ref, dense_ref, w_ref,
    table, owner_live, acc, index_out, index_in, index_smem, gather0, gather1,
    send_c, total, recv_c, recv_ax, recv_ay, recv_by, recv_bx, recv_z,
    owner_sem, row_sem, len_sem, dense_sem, w_sem,
    table_sem, index_send_sem, index_recv_sem, own_sem, smem_sem,
    send_c_sem, send_ax_sem, send_ay_sem, send_by_sem, send_bx_sem, send_z_sem,
    recv_c_sem, recv_ax_sem, recv_ay_sem, recv_by_sem, recv_bx_sem, recv_z_sem,
):
    nz, ncol, ny, nx, nc, cap = sizes
    owners = nz * ncol
    hist, users = owner_ref.shape
    half = users // 2
    width = acc.shape[0]
    tiles = width // LANES
    cap_rows = round_up(cap, 16)
    z = lax.axis_index("row")
    col = lax.axis_index("col")
    me = z * ncol + col
    c = col % nc
    x = (col // nc) % nx
    y = col // (nc * nx)

    def column(y_at, x_at, c_at):
        return (y_at * nx + x_at) * nc + c_at

    small = [
        pltpu.make_async_copy(*refs)
        for refs in (
            (len_hbm, len_ref, len_sem), (owner_hbm, owner_ref, owner_sem),
            (row_hbm, row_ref, row_sem), (dense_hbm, dense_ref, dense_sem),
            (w_hbm, w_ref, w_sem),
        )
    ]
    for copy in small:
        copy.start()

    pieces = 8
    piece = table.shape[0] // pieces
    for at in range(pieces):
        rows = pl.ds(at * piece, piece)
        pltpu.make_async_copy(table_hbm.at[rows], table.at[rows], table_sem).start()

    barrier = pltpu.get_barrier_semaphore()

    @pl.loop(1, owners)
    def _(step):
        there = lax.rem(me + step, owners)
        pl.semaphore_signal(
            barrier, inc=1, device_id=(there // ncol, lax.rem(there, ncol)), device_id_type=MESH
        )

    for copy in small[:3]:
        copy.wait()
    lengths = len_ref[...]
    position = lax.broadcasted_iota(jnp.int32, (hist, users), 0)
    owner_live[...] = jnp.where(position < lengths, owner_ref[...], -1)
    owner_iota = lax.broadcasted_iota(jnp.int32, (owners, users), 0)

    def count(at, carry):
        return carry + jnp.where(owner_live[pl.ds(at, 1), :] == owner_iota, 1.0, 0.0)

    per_user = lax.fori_loop(0, hist, count, jnp.zeros((owners, users), jnp.float32), unroll=5)
    before = lax.broadcasted_iota(jnp.int32, (users, users), 0) < lax.broadcasted_iota(
        jnp.int32, (users, users), 1
    )
    offsets = jnp.dot(
        per_user.astype(jnp.bfloat16),
        jnp.where(before, 1.0, 0.0).astype(jnp.bfloat16),
        preferred_element_type=jnp.float32,
    )
    acc[...] = jnp.zeros_like(acc)
    slot_iota = lax.broadcasted_iota(jnp.int32, (cap_rows, users), 0).astype(jnp.float32)
    user_number = lax.broadcasted_iota(jnp.int32, (1, users), 1).astype(jnp.float32) + 1.0
    group = 5 if hist % 5 == 0 else 1

    def place(step, counts):
        left, right = [], []
        for k in range(group):
            at = step * group + k
            row_id = row_ref[pl.ds(at, 1), :]
            high = row_id >> 8
            low = (row_id & 255).astype(jnp.float32)
            high = high.astype(jnp.float32)
            match = owner_live[pl.ds(at, 1), :] == owner_iota
            rank = jnp.sum(jnp.where(match, counts, 0.0), axis=0, keepdims=True)
            counts = counts + jnp.where(match, 1.0, 0.0)
            right.append(jnp.where(slot_iota == rank, 1.0, 0.0).astype(jnp.bfloat16))
            values = [jnp.where(match, v, 0.0) for v in (high, low, user_number)]
            left.append(jnp.concatenate(values, axis=0).astype(jnp.bfloat16))
        acc[:cap_rows, :3 * owners] += lax.dot_general(
            jnp.concatenate(right, axis=1),
            jnp.concatenate(left, axis=1),
            (((1,), (1,)), ((), ())),
            preferred_element_type=jnp.float32,
        )
        return counts

    lax.fori_loop(0, hist // group, place, offsets)
    for at in range(tiles):
        found = acc[at * LANES:(at + 1) * LANES, :].T
        rows = found[0:owners] * 256.0 + found[owners:2 * owners]
        index_out[:, at, :] = jnp.clip(rows.astype(jnp.int32), 0, table.shape[0] - 1)
        index_out[:, tiles + at, :] = found[2 * owners:3 * owners].astype(jnp.int32)

    pl.semaphore_wait(barrier, owners - 1)

    @pl.loop(1, owners)
    def _(step):
        there = lax.rem(me + step, owners)
        pltpu.make_async_remote_copy(
            src_ref=index_out.at[there],
            dst_ref=index_in.at[me],
            send_sem=index_send_sem,
            recv_sem=index_recv_sem,
            device_id=(there // ncol, lax.rem(there, ncol)),
            device_id_type=MESH,
        ).start()

    own = pltpu.make_async_copy(index_out.at[me], index_in.at[me], own_sem)
    own.start()

    for copy in small[3:]:
        copy.wait()
    hidden = jnp.dot(dense_ref[...], w_ref[...], preferred_element_type=jnp.float32)
    dim = pooled_ref.shape[1]
    silu_ref[...] = hidden / (1.0 + jnp.exp(-hidden))
    gather0[...] = jnp.zeros_like(gather0)
    gather1[...] = jnp.zeros_like(gather1)

    own.wait()
    drain(index_in.at[pl.ds(0, owners - 1)], index_recv_sem)
    to_smem = pltpu.make_async_copy(index_in, index_smem, smem_sem)
    to_smem.start()
    to_smem.wait()
    drain(table, table_sem)

    user_iota = lax.broadcasted_iota(jnp.int32, (users, LANES), 0) + 1

    batch = 24

    def fetch(source, gathered):
        for first in range(0, cap, batch):
            slots = range(first, min(first + batch, cap))
            found = [
                table[pl.ds(index_smem[source, slot // LANES, slot % LANES], 1), :]
                for slot in slots
            ]
            for slot, row in zip(slots, found):
                gathered[slot:slot + 1, :] = row

    def block_sum(source, gathered):
        names = [index_in[source, pl.ds(tiles + at, 1), :] for at in range(tiles)]
        select = jnp.concatenate(
            [jnp.where(name == user_iota, 1.0, 0.0).astype(jnp.bfloat16) for name in names], axis=1
        )
        values = gathered[...]
        high = values.astype(jnp.bfloat16)
        low = (values - high.astype(jnp.float32)).astype(jnp.bfloat16)
        both = jnp.dot(
            select, jnp.concatenate([high, low], axis=1), preferred_element_type=jnp.float32
        )
        return both[:, :dim] + both[:, dim:]

    def send(src, dst, send_sem, recv_sem, z_at, col_at):
        pltpu.make_async_remote_copy(
            src_ref=src, dst_ref=dst, send_sem=send_sem, recv_sem=recv_sem,
            device_id=(z_at, col_at), device_id_type=MESH,
        ).start()

    def source_of(dx, dy, dz):
        return lax.rem(z + dz, nz) * ncol + column(lax.rem(y + dy, ny), lax.rem(x + dx, nx), 0)

    def offsets_at(step):
        group = step // nz
        return nx - 1 - group % nx, ny - 1 - group // nx, (step + 1) % nz

    def compute(step):
        dx, dy, dz = offsets_at(step)
        slot = (dy * nx + dx) * nz + dz
        base = source_of(dx, dy, dz)
        send_c[slot] = block_sum(base + 1 - c, gather0)
        fetch(base + c, gather1)
        send(send_c.at[slot], recv_c.at[slot], send_c_sem, recv_c_sem.at[slot],
             z, column(y, x, 1 - c))
        total[slot] = block_sum(base + c, gather1)
        fetch(source_of(*offsets_at((step + 1) % chips)) + 1 - c, gather0)

    def combine(step):
        dx, dy, dz = offsets_at(step)
        yt, xt = lax.rem(y + dy, ny), lax.rem(x + dx, nx)
        slot = (dy * nx + dx) * nz + dz
        drain(recv_c.at[slot], recv_c_sem.at[slot])
        total[slot] += recv_c[slot]
        near_x, near_y = dx == 0, dy == 0
        both = jnp.logical_and(near_x, near_y)
        upper, lower = pl.ds(0, half), pl.ds(half, half)

        def add(part, landed, sem, at):
            drain(landed.at[at], sem.at[at])
            total[slot, part] += landed[at]

        @pl.when(near_x)
        def _():
            for k in range(nx - 1):
                add(upper, recv_ax, recv_ax_sem, (k * ny + dy) * nz + dz)

        @pl.when(near_y)
        def _():
            for k in range(ny - 1):
                add(lower, recv_by, recv_by_sem, (k * nx + dx) * nz + dz)

        @pl.when(both)
        def _():
            for k in range(ny - 1):
                add(upper, recv_ay, recv_ay_sem, k * nz + dz)
            for k in range(nx - 1):
                add(lower, recv_bx, recv_bx_sem, k * nz + dz)

        @pl.when(dx > 0)
        def _():
            at = ((dx - 1) * ny + dy) * nz + dz
            send(total.at[slot, upper], recv_ax.at[at], send_ax_sem, recv_ax_sem.at[at],
                 z, column(y, xt, c))

        @pl.when(dy > 0)
        def _():
            at = ((dy - 1) * nx + dx) * nz + dz
            send(total.at[slot, lower], recv_by.at[at], send_by_sem, recv_by_sem.at[at],
                 z, column(yt, x, c))

        @pl.when(jnp.logical_and(near_x, dy > 0))
        def _():
            at = (dy - 1) * nz + dz
            send(total.at[slot, upper], recv_ay.at[at], send_ay_sem, recv_ay_sem.at[at],
                 z, column(yt, x, c))

        @pl.when(jnp.logical_and(near_y, dx > 0))
        def _():
            at = (dx - 1) * nz + dz
            send(total.at[slot, lower], recv_bx.at[at], send_bx_sem, recv_bx_sem.at[at],
                 z, column(y, xt, c))

        @pl.when(jnp.logical_and(both, dz > 0))
        def _():
            send(total.at[dz], recv_z.at[dz - 1], send_z_sem, recv_z_sem.at[dz - 1],
                 lax.rem(z + dz, nz), col)

    chips = nz * ny * nx
    fetch(source_of(*offsets_at(0)) + 1 - c, gather0)

    delay = min(3, chips)

    @pl.loop(0, chips + delay)
    def _(step):
        @pl.when(step < chips)
        def _():
            compute(step)

        @pl.when(step >= delay)
        def _():
            combine(step - delay)

    pooled = total[0]
    for k in range(nz - 1):
        drain(recv_z.at[k], recv_z_sem.at[k])
        pooled = pooled + recv_z[k]
    divisor = jnp.broadcast_to(lengths.astype(jnp.float32), (users, users)).T
    pooled_ref[...] = pooled / divisor[:, :1]

    drain(index_in.at[pl.ds(0, owners - 1)], index_send_sem)
    drain(send_c, send_c_sem)
    drain(recv_ax, send_ax_sem)
    drain(recv_ay, send_ay_sem)
    drain(recv_by, send_by_sem)
    drain(recv_bx, send_bx_sem)
    drain(recv_z, send_z_sem)


def per_device(nz, ncol, item_table, owner_ids, row_ids, lengths, dense_input, w_bottom):
    users, hist = owner_ids.shape
    rows, dim = item_table.shape
    owners = nz * ncol
    cap = 3 * users * hist // (2 * owners)
    width = round_up(cap, LANES)
    tile_rows = round_up(2 * (width // LANES), SUBLANES)
    nc, nx = 2, 2
    ny = ncol // (nc * nx)
    chips = nz * ny * nx
    half = users // 2
    ax, ay, by, bx = (nx - 1) * ny * nz, (ny - 1) * nz, (ny - 1) * nx * nz, (nx - 1) * nz
    dma = pltpu.SemaphoreType.DMA
    vmem = pl.BlockSpec(memory_space=pltpu.VMEM)

    def floats(*shape):
        return pltpu.VMEM(shape, jnp.float32)

    pooled, dense_out = pl.pallas_call(
        functools.partial(kernel, (nz, ncol, ny, nx, nc, cap)),
        out_shape=[
            jax.ShapeDtypeStruct((users, dim), jnp.float32),
            jax.ShapeDtypeStruct((users, w_bottom.shape[1]), jnp.float32),
        ],
        in_specs=[pl.BlockSpec(memory_space=pl.ANY)] * 6,
        out_specs=[vmem, vmem],
        scratch_shapes=[
            pltpu.VMEM((hist, users), jnp.int32),
            pltpu.VMEM((hist, users), jnp.int32),
            pltpu.VMEM((1, users), jnp.int32),
            pltpu.VMEM(dense_input.shape, dense_input.dtype),
            pltpu.VMEM(w_bottom.shape, w_bottom.dtype),
            floats(rows, dim),
            pltpu.VMEM((hist, users), jnp.int32),
            floats(width, round_up(3 * owners, LANES)),
            pltpu.VMEM((owners, tile_rows, LANES), jnp.int32),
            pltpu.VMEM((owners, tile_rows, LANES), jnp.int32),
            pltpu.SMEM((owners, tile_rows, LANES), jnp.int32),
            floats(width, dim),
            floats(width, dim),
            floats(chips, users, dim),
            floats(chips, users, dim),
            floats(chips, users, dim),
            floats(ax, half, dim),
            floats(ay, half, dim),
            floats(by, half, dim),
            floats(bx, half, dim),
            floats(nz - 1, users, dim),
        ]
        + [dma] * 16
        + [dma((chips,)), dma((ax,)), dma((ay,)), dma((by,)), dma((bx,)), dma((nz - 1,))],
        compiler_params=pltpu.CompilerParams(
            collective_id=0, has_side_effects=True, vmem_limit_bytes=56 * 1024 * 1024
        ),
    )(item_table, owner_ids.T, row_ids.T, lengths[None, :], dense_input, w_bottom)
    return jnp.concatenate([pooled, dense_out], axis=1)


def solution(mesh):
    in_specs = (
        P(("row", "col"), None),
        P(("row", "col"), None),
        P(("row", "col"), None),
        P(("row", "col")),
        P(("row", "col"), None),
        P(),
    )
    out_specs = P(("row", "col"), None)
    body = functools.partial(per_device, mesh.shape["row"], mesh.shape["col"])
    return jax.shard_map(
        body, mesh=mesh, in_specs=in_specs, out_specs=out_specs, check_vma=False
    )
```
